32 devices in a mesh: seq: 8 (over y, x, core), mp: 4 (over z).
Axes of the slice: x: 2, y: 2, z: 4, core: 2. Of those that a mesh axis runs over, the one named last changes fastest.
Arguments:
- queries: bfloat16 [1024, 2048], P('seq', 'mp'), may hold values from -2 to 2
- keys: bfloat16 [1024, 2048], P('seq', 'mp'), may hold values from -2 to 2
- values: bfloat16 [1024, 2048], P('seq', 'mp'), may hold values from -6 to 6
- log_decay: float32 [16, 1024], P('mp', 'seq'), may hold values from -1.2 to 0
- residual: bfloat16 [1024, 6144], P(('seq', 'mp')), may hold values from -6 to 6
- out_weight: bfloat16 [2048, 6144], P('mp', 'seq'), may hold values from -0.125 to 0.125
- gate_weight: bfloat16 [8, 6144, 2304], P('seq', None, 'mp'), may hold values from -0.078125 to 0.078125
- up_weight: bfloat16 [8, 6144, 2304], P('seq', None, 'mp'), may hold values from -0.078125 to 0.078125
- down_weight: bfloat16 [8, 2304, 6144], P('seq', 'mp'), may hold values from -0.09375 to 0.09375
- expert_ids: int32 [1024, 2], P(('seq', 'mp')), may hold values from 0 to 3, all different within a row; in each aligned block of 32 rows (0 to 31, 32 to 63, ...) at most 24 rows name the same one
- route_weights: float32 [1024, 2], P(('seq', 'mp')), may hold values from 0.2 to 1
Outputs:
- output: bfloat16 [1024, 6144], P(('seq', 'mp'))
The draws below stay inside these ranges and needn't reach their ends.
Inputs may be any that keep to these rules, and one draw needn't show every extreme that they name: `expert_ids`: the 2 experts of a token differ. Among the 32 tokens of one device (aligned blocks of rows in token order) no expert is named more than 24 times, a bound that some block reaches.
All inputs are finite; a program needn't handle non-finite values.
Results may differ from the reference program's by a relative error of at most 0.015.
Values may be sent and summed in bfloat16 or wider, within the bound.
No kernel may reach another device: no remote copies, remote signals or barrier semaphores. Data moves between devices by JAX's collectives and lax.ppermute only.
A program may use at most 128 MiB of HBM per device.

```python
import math
import jax
import jax.numpy as jnp
import numpy as np
from jax import lax

D = 6144
HD = 128
TOP = 2
HEAD_DEV = 4
FE = 4608
PAIR = 2
TOK_SEQ = 128
HEADS = 16
EXPERTS = 4
TOKEN_COUNT = 1024
TOK_DEV = 32
CAP = 24
N_SEQ = 8
N_MP = 4


def draw_log_decay(key, part):
    every_key_row = jax.random.split(key, 7)
    slow_share = 5
    slow_heads = jax.random.randint(every_key_row[0], (HEADS, 1), 0, 10) < slow_share
    slow_rate = jax.random.uniform(every_key_row[1], (HEADS, 1), jnp.float32, 0.1, 0.5) / TOKEN_COUNT
    fast_rate = jax.random.uniform(every_key_row[2], (HEADS, 1), jnp.float32, 1.0 / 50.0, 1.0 / 30.0)
    baseline_decay_rate = jnp.where(slow_heads, slow_rate, fast_rate)
    window_multiplier = jnp.exp(jax.random.uniform(every_key_row[3], (HEADS, TOKEN_COUNT // TOK_SEQ, 1), jnp.float32, math.log(0.6), math.log(1.5)))
    window_multiplier = jnp.broadcast_to(window_multiplier, (HEADS, TOKEN_COUNT // TOK_SEQ, TOK_SEQ)).reshape(HEADS, TOKEN_COUNT)
    random_perturbation = jax.random.uniform(every_key_row[4], (HEADS, TOKEN_COUNT), jnp.float32, 0.6, 1.4)
    spike_positions = jax.random.randint(every_key_row[5], (2,), 0, TOKEN_COUNT)
    retained_fraction = jax.random.uniform(every_key_row[6], (2,), jnp.float32, 0.6, 0.8)
    position_indices = jnp.arange(TOKEN_COUNT)
    spike_log_decay = jnp.sum(jnp.where(position_indices[None, :] == spike_positions[:, None], jnp.log(retained_fraction)[:, None], 0.0), axis=0)
    return -baseline_decay_rate * window_multiplier * random_perturbation + spike_log_decay[None, :]


def block_scale(rng, shape, cuts, least, largest):
    def one(position, blocks):
        steps = jax.random.uniform(jax.random.fold_in(jax.random.fold_in(rng, 6), position), (blocks,), jnp.float32, least / len(cuts), largest / len(cuts))
        return jnp.repeat(jnp.exp(steps), shape[position] // blocks).reshape((-1,) + (1,) * (len(shape) - position - 1))

    gain = one(*cuts[0])
    for cut in cuts[1:]:
        gain = gain * one(*cut)
    return gain


def shared_out(key, own, number, rows, count, top, reach, skew):
    sequence = jax.random.permutation(key, count)
    heavy_load, usual = load_shares(count, rows * top, reach, skew, True), load_shares(count, rows * top, reach, skew, False)
    places = jnp.arange(count)

    def named(lengths, turn):
        used = int((lengths > 0).sum())
        fixed = max(1, used // 4)
        shifted = fixed + (places - fixed + turn * (used - fixed)) % max(1, count - fixed)
        return jnp.zeros((count,), jnp.int32).at[sequence[jnp.where(places < fixed, places, shifted)]].set(jnp.asarray(lengths, jnp.int32))

    lengths = jnp.where(number % 4 == 0, named(heavy_load, number // 4), named(usual, number - number // 4 - 1))
    mixed = jax.random.permutation(jax.random.fold_in(own, 3), count)
    source_of, taker = mixed[0:count // 2 * 2:2], mixed[1:count // 2 * 2:2]
    room = jnp.minimum(lengths[source_of] - 1, reach - lengths[taker]) // 2
    room = jnp.where((source_of == sequence[0]) | (taker == sequence[0]) | (lengths[taker] == 0), 0, jnp.maximum(room, 0))
    shifted = jax.random.randint(jax.random.fold_in(own, 4), (count // 2,), 0, 1 << 20) % (room + 1)
    lengths = lengths.at[source_of].add(-shifted).at[taker].add(shifted)
    items = jnp.searchsorted(jnp.cumsum(lengths), jnp.arange(rows * top), side="right").astype(jnp.int32)
    grid = items.reshape(top, rows).T
    grid = grid[jax.random.permutation(jax.random.fold_in(own, 1), rows)]
    turn = jax.random.randint(jax.random.fold_in(own, 2), (rows, 1), 0, top)
    return jnp.take_along_axis(grid, (jnp.arange(top)[None, :] + turn) % top, axis=1)


def load_shares(count, total, most, slope, full):
    portions = [(1 << 20) // math.isqrt(standing ** slope) + 1 for standing in range(1, count + 1)]
    largest = most if full else min(most, max(-(-total // count), total * portions[0] // sum(portions)))
    least = 1 if total - largest >= count - 1 else 0
    counts, surplus = [largest] + [least] * (count - 1), total - largest - least * (count - 1)
    while surplus > 0:
        candidates = [i for i in range(1, count) if counts[i] < largest] or [i for i in range(1, count) if counts[i] < most]
        pool, left = sum([portions[i] for i in candidates]), surplus
        for i in candidates:
            extra = min(most - counts[i], max(1, left * portions[i] // pool), surplus)
            counts[i] = counts[i] + extra
            surplus = surplus - extra
    return np.array(counts)


def bell_draw(rng, extent, deviation, bound, cuts=(), held_as=jnp.bfloat16):
    values = deviation * jax.random.normal(rng, extent, jnp.float32)
    if cuts:
        values = values * block_scale(rng, extent, cuts, -0.22, 0.18)
    return jnp.clip(values, -bound, bound).astype(held_as)


def setup_inputs(seed: int = 0) -> dict:
    streams_of = jax.random.split(jax.random.key(seed), 12)
    queries = bell_draw(streams_of[0], (TOKEN_COUNT, HEADS * HD), 0.3, 2.0, ((0, 8), (1, 4)))
    keys = bell_draw(streams_of[1], (TOKEN_COUNT, HEADS * HD), 0.3, 2.0, ((0, 8), (1, 4)))
    values = bell_draw(streams_of[2], (TOKEN_COUNT, HEADS * HD), 1.0, 6.0, ((0, 8), (1, 4)))
    log_decay = draw_log_decay(jax.random.fold_in(streams_of[11], 71), 0)
    residual = bell_draw(streams_of[4], (TOKEN_COUNT, D), 1.0, 6.0, ((0, 32),))
    out_weight = bell_draw(streams_of[5], (HEADS * HD, D), (HEADS * HD) ** -0.5, 0.125, ((0, 4), (1, 8)))
    gate_weight = bell_draw(streams_of[6], (EXPERTS * PAIR, D, FE // PAIR), D ** -0.5, 0.078125, ((0, 8), (2, 4)))
    up_weight = bell_draw(streams_of[7], (EXPERTS * PAIR, D, FE // PAIR), D ** -0.5, 0.078125, ((0, 8), (2, 4)))
    down_weight = bell_draw(streams_of[8], (EXPERTS * PAIR, FE // PAIR, D), FE ** -0.5, 0.09375, ((0, 8), (1, 4)))
    expert_ids_keys = jax.random.split(jax.random.fold_in(streams_of[9], 1), TOKEN_COUNT // TOK_DEV)
    expert_ids_turns = jax.random.permutation(jax.random.fold_in(streams_of[9], 3), TOKEN_COUNT // TOK_DEV)
    expert_ids = jax.vmap(lambda own, number: shared_out(jax.random.fold_in(streams_of[9], 2), own, number, TOK_DEV, EXPERTS, TOP, CAP, 1))(expert_ids_keys, expert_ids_turns).reshape((TOKEN_COUNT, TOP))
    route_weights = jnp.clip(0.2 + 0.8 * jax.random.uniform(streams_of[10], (TOKEN_COUNT, TOP), jnp.float32) ** block_scale(streams_of[10], (TOKEN_COUNT, TOP), ((0, 32),), -0.2, 0.2), 0.2, 1.0)
    return {"queries": queries, "keys": keys, "values": values, "log_decay": log_decay, "residual": residual, "out_weight": out_weight, "gate_weight": gate_weight, "up_weight": up_weight, "down_weight": down_weight, "expert_ids": expert_ids, "route_weights": route_weights}


def round_low(array):
    return lax.optimization_barrier(array.astype(jnp.bfloat16)).astype(jnp.float32)

def reference(queries, keys, values, log_decay, residual, out_weight, gate_weight, up_weight, down_weight, expert_ids, route_weights):
    query_heads = queries.reshape(N_SEQ, TOK_SEQ, HEADS, HD).astype(jnp.float32)
    key_heads = keys.reshape(N_SEQ, TOK_SEQ, HEADS, HD).astype(jnp.float32)
    value_heads = values.reshape(N_SEQ, TOK_SEQ, HEADS, HD).astype(jnp.float32)
    cumulative = jnp.cumsum(log_decay.reshape(HEADS, N_SEQ, TOK_SEQ), axis=2).transpose(1, 0, 2)
    positions = jnp.arange(TOK_SEQ)
    causal = positions[:, None] >= positions[None, :]
    spread_log = cumulative[:, :, :, None] - cumulative[:, :, None, :]
    weight = jnp.where(causal, jnp.exp(jnp.where(causal, spread_log, 0.0)), 0.0)
    raw_scores = jnp.einsum('cthd,cshd->chts', query_heads, key_heads)
    local_scores = round_low(raw_scores * weight)
    local_part = jnp.einsum('chts,cshd->cthd', local_scores, value_heads)
    span_total = cumulative[:, :, -1]
    key_scale = jnp.exp(span_total[:, :, None] - cumulative)
    weighted_keys = round_low(key_scale.transpose(0, 2, 1)[..., None] * key_heads)
    span_state = round_low(jnp.einsum('cthd,cthe->chde', weighted_keys, value_heads))

    def advance(carry_state, inputs):
        log_total, state_now = inputs
        return (jnp.exp(log_total)[:, None, None] * carry_state + state_now, carry_state)
    empty_state = jnp.zeros((HEADS, HD, HD), jnp.float32)
    final_state, prefixes = lax.scan(advance, empty_state, (span_total, span_state))
    weighted_queries = round_low(jnp.exp(cumulative).transpose(0, 2, 1)[..., None] * query_heads)
    carried_part = jnp.einsum('cthd,chde->cthe', weighted_queries, round_low(prefixes))
    mixed_heads = local_part + carried_part
    normed = (mixed_heads * lax.rsqrt(lax.optimization_barrier(jnp.mean(mixed_heads * mixed_heads, axis=-1, keepdims=True)) + 1e-06)).astype(jnp.bfloat16)
    normed = normed.reshape(TOKEN_COUNT, HEADS * HD)
    group_rows = normed.reshape(TOKEN_COUNT, N_MP, HEAD_DEV * HD)
    group_weights = out_weight.reshape(N_MP, HEAD_DEV * HD, D)

    def add_group(total_sum, group_index):
        part = jnp.dot(group_rows[:, group_index, :], group_weights[group_index], preferred_element_type=jnp.float32)
        return (total_sum + round_low(part), group_index)
    projected, unused = lax.scan(add_group, jnp.zeros((TOKEN_COUNT, D), jnp.float32), jnp.arange(N_MP, dtype=jnp.int32))
    hidden_state = (residual.astype(jnp.float32) + projected).astype(jnp.bfloat16)
    hidden_wide = hidden_state.astype(jnp.float32)
    moe_input = (hidden_wide * lax.rsqrt(lax.optimization_barrier(jnp.mean(hidden_wide * hidden_wide, axis=-1, keepdims=True)) + 1e-06)).astype(jnp.bfloat16)
    flat_ids = expert_ids.reshape(-1)
    assign_count = TOKEN_COUNT * TOP
    expert_hot = (flat_ids[:, None] == jnp.arange(EXPERTS, dtype=jnp.int32)[None, :]).astype(jnp.int32)
    slot_rank = lax.optimization_barrier(jnp.sum((jnp.cumsum(expert_hot, axis=0) - expert_hot) * expert_hot, axis=1)).astype(jnp.int32)
    owners = (jnp.arange(assign_count, dtype=jnp.int32) // TOP).astype(jnp.int32)
    most_rows = N_SEQ * N_MP * CAP
    slot_table = jnp.zeros((EXPERTS, most_rows), jnp.int32).at[flat_ids, slot_rank].set(owners)
    slice_width = FE // (PAIR * N_MP)
    gate_split = gate_weight.reshape(EXPERTS, PAIR, D, N_MP, slice_width)
    up_split = up_weight.reshape(EXPERTS, PAIR, D, N_MP, slice_width)
    down_split = down_weight.reshape(EXPERTS, PAIR, N_MP, slice_width, D)

    def run_expert(expert):
        expert_rows = moe_input[slot_table[expert]]
        total_sum = jnp.zeros((most_rows, D), jnp.float32)
        for half_index in range(PAIR):
            running_sum = jnp.zeros((most_rows, D), jnp.float32)
            for group_index in range(N_MP):
                gate_value = jnp.dot(expert_rows, gate_split[expert, half_index, :, group_index, :], preferred_element_type=jnp.float32)
                lifted = jnp.dot(expert_rows, up_split[expert, half_index, :, group_index, :], preferred_element_type=jnp.float32)
                expert_hidden = (jax.nn.silu(gate_value) * lifted).astype(jnp.bfloat16)
                slice_out = jnp.dot(expert_hidden, down_split[expert, half_index, group_index], preferred_element_type=jnp.float32)
                running_sum = running_sum + round_low(slice_out)
            total_sum = total_sum + round_low(running_sum)
        return total_sum
    results = lax.map(run_expert, jnp.arange(EXPERTS, dtype=jnp.int32))
    picked = results[flat_ids, slot_rank].reshape(TOKEN_COUNT, TOP, D)
    expert_mix = lax.optimization_barrier(jnp.sum(route_weights[:, :, None] * picked, axis=1))
    return (hidden_wide + expert_mix).astype(jnp.bfloat16)
```

```python
import functools

import jax
import jax.numpy as jnp
from jax import lax
from jax.experimental import pallas as pl
from jax.experimental.pallas import tpu as pltpu
from jax.sharding import PartitionSpec as P

TOP = 2
PAIR = 2
VMEM_LIMIT = 44 * 1024 * 1024
DECAY_ROWS = 16
HIGH = lax.Precision.HIGHEST
F32 = jnp.float32
BF16 = jnp.bfloat16


def params():
    return pltpu.CompilerParams(vmem_limit_bytes=VMEM_LIMIT)


def cost(flops, moved):
    return pl.CostEstimate(flops=int(flops), bytes_accessed=int(moved), transcendentals=0)


def after(array, *earlier):
    return lax.optimization_barrier((array,) + earlier)[0]


def swap_columns(array, distance):
    count = lax.axis_size("seq")
    return lax.ppermute(array, "seq", [(i, i ^ (PAIR * distance)) for i in range(count)])


def swap_cores(array):
    count = lax.axis_size("seq")
    return lax.ppermute(array, "seq", [(i, i ^ 1) for i in range(count)])


def swap_layers(array, distance):
    count = lax.axis_size("mp")
    return lax.ppermute(array, "mp", [(i, i ^ distance) for i in range(count)])


def local_kernel(q_ref, k_ref, v_ref, decay_ref, state_ref, local_ref, weighted_ref):
    span = q_ref.shape[0]
    heads = decay_ref.shape[0]
    size = q_ref.shape[1] // heads
    row = lax.broadcasted_iota(jnp.int32, (span, span), 0)
    col = lax.broadcasted_iota(jnp.int32, (span, span), 1)
    causal = row >= col
    decay = decay_ref[...]
    along = jnp.dot(decay, (row <= col).astype(F32), precision=HIGH, preferred_element_type=F32)
    down = lax.dot_general(
        causal.astype(F32), decay, (((1,), (1,)), ((), ())), precision=HIGH, preferred_element_type=F32
    )
    extra = lax.broadcasted_iota(jnp.int32, (DECAY_ROWS, size), 0)
    for h in range(heads):
        cols = slice(h * size, (h + 1) * size)
        q, k, v = q_ref[:, cols], k_ref[:, cols], v_ref[:, cols]
        here = down[:, h : h + 1]
        spread = here - along[h : h + 1, :]
        weight = jnp.where(causal, jnp.exp(jnp.where(causal, spread, 0.0)), 0.0)
        raw = lax.dot_general(q, k, (((1,), (1,)), ((), ())), preferred_element_type=F32)
        local_ref[:, cols] = jnp.dot((raw * weight).astype(BF16), v, preferred_element_type=F32)
        total = along[h : h + 1, span - 1 : span]
        scaled = (jnp.exp(total - here) * k.astype(F32)).astype(BF16)
        state_ref[h, :size, :] = lax.dot_general(
            scaled, v, (((0,), (0,)), ((), ())), preferred_element_type=F32
        ).astype(BF16)
        first = total.astype(BF16).astype(F32)
        second = (total - first).astype(BF16).astype(F32)
        third = total - first - second
        pieces = jnp.where(extra == 0, first, jnp.where(extra == 1, second, jnp.where(extra == 2, third, 0.0)))
        state_ref[h, size:, :] = pieces.astype(BF16)
        weighted_ref[:, cols] = (jnp.exp(here) * q.astype(F32)).astype(BF16)


def prefix_kernel(count, layers, *refs):
    row_ref, between_ref, earlier_ref, local_ref, weighted_ref = refs[:5]
    state_refs = refs[5 : 5 + count]
    out_ref, totals, held = refs[5 + count :]
    heads, tall, size = state_refs[0].shape
    span = local_ref.shape[0]
    for p in range(count):
        for h in range(heads):
            totals[p : p + 1, h * size : (h + 1) * size] = jnp.sum(
                state_refs[p][h, size:, :].astype(F32), axis=0, keepdims=True
            )
    gap = jnp.dot(between_ref[...], totals[...], precision=HIGH, preferred_element_type=F32)
    totals[...] = jnp.exp(gap) * earlier_ref[...]
    for h in range(heads):
        cols = slice(h * size, (h + 1) * size)
        prefix = jnp.zeros((size, size), F32)
        for p in range(count):
            prefix += totals[p : p + 1, cols] * state_refs[p][h, :size, :].astype(F32)
        mixed = local_ref[:, cols] + jnp.dot(
            weighted_ref[:, cols], prefix.astype(BF16), preferred_element_type=F32
        )
        mean = jnp.mean(mixed * mixed, axis=-1, keepdims=True)
        held[:, cols] = (mixed * lax.rsqrt(mean + 1e-06)).astype(BF16)
    rows = span // layers
    for r in range(layers):
        start = pl.multiple_of(row_ref[r] * rows, rows)
        out_ref[r * rows : (r + 1) * rows, :] = held[pl.ds(start, rows), :]


def project_kernel(count, *refs):
    place_ref, rows_ref = refs[:2]
    weight_refs = refs[2 : 2 + count]
    keep_ref, send_ref = refs[2 + count :]
    half = keep_ref.shape[0]
    width = weight_refs[0].shape[1]
    rows = rows_ref[...]
    for p in range(count):
        part = jnp.dot(rows, weight_refs[p][...], preferred_element_type=F32).astype(BF16)
        start = pl.multiple_of(place_ref[p] * width, width)
        keep_ref[:, pl.ds(start, width)] = part[:half]
        send_ref[:, pl.ds(start, width)] = part[half:]


def pack_kernel(count, map_ref, near_ref, far_ref, *out_refs):
    rows = out_refs[0].shape[0]
    tokens = jnp.concatenate([near_ref[...], far_ref[...]], axis=0)
    packed = jnp.dot(map_ref[...], tokens, preferred_element_type=F32).astype(BF16)
    for d in range(count):
        out_refs[d][...] = packed[d * rows : (d + 1) * rows]


def expert_kernel(pieces, blocks, first, last, features, *refs):
    x_refs = refs[:pieces]
    gate_refs, up_refs = refs[pieces : pieces + blocks], refs[pieces + blocks : pieces + 2 * blocks]
    rest = refs[pieces + 2 * blocks :]
    if not first:
        sum_in, square_in = rest[:2]
        rest = rest[2:]
    if last:
        out_ref, sum_ref, square_ref = rest
    else:
        sum_ref, square_ref = rest
    size = gate_refs[0].shape[0]
    even = size // 128 * 128
    step = pl.program_id(0)
    x = jnp.concatenate([ref[...] for ref in x_refs], axis=0)
    gate = jnp.concatenate([ref[...] for ref in gate_refs], axis=1)
    up = jnp.concatenate([ref[...] for ref in up_refs], axis=1)
    both = jnp.concatenate([gate[:even], up[:even], gate[even:], up[even:]], axis=0)
    sums = lax.dot_general(x, both, (((1,), (1,)), ((), ())), preferred_element_type=F32)
    wide = x.astype(F32)
    lanes = square_ref.shape[1]
    squares = wide[:, :lanes] * wide[:, :lanes]
    for i in range(1, x.shape[1] // lanes):
        part = wide[:, i * lanes : (i + 1) * lanes]
        squares += part * part

    @pl.when(step == 0)
    def _():
        sum_ref[...] = sums if first else sum_in[...] + sums
        square_ref[...] = squares if first else square_in[...] + squares

    @pl.when(step > 0)
    def _():
        sum_ref[...] += sums
        square_ref[...] += squares

    if last:

        @pl.when(step == pl.num_programs(0) - 1)
        def _():
            mean = jnp.sum(square_ref[...], axis=1, keepdims=True) / features
            scale = lax.rsqrt(mean + 1e-06)

            def activate(gate, up):
                gate = gate * scale
                return (gate / (1.0 + jnp.exp(-gate)) * (up * scale)).astype(BF16)

            out_ref[:, :even] = activate(sum_ref[:, :even], sum_ref[:, even : 2 * even])
            if even < size:
                tail = sum_ref[:, 2 * even :]
                out_ref[:, even:] = activate(tail[:, : size - even], tail[:, size - even :])


def down_kernel(hidden_ref, weight_ref, own_ref, other_ref):
    half = own_ref.shape[0]
    out = jnp.dot(hidden_ref[...], weight_ref[...], preferred_element_type=F32).astype(BF16)
    own_ref[...] = out[:half]
    other_ref[...] = out[half:]


def combine_kernel(count, high_ref, low_ref, *refs):
    x_refs = refs[:count]
    keep_ref, send_ref = refs[count:]
    half = keep_ref.shape[0]
    x = jnp.concatenate([ref[...] for ref in x_refs], axis=0)
    out = jnp.dot(high_ref[...], x, preferred_element_type=F32)
    out += jnp.dot(low_ref[...], x, preferred_element_type=F32)
    keep_ref[...] = out[:half]
    send_ref[...] = out[half:].astype(BF16)


def whole_block(array):
    return pl.BlockSpec(array.shape, lambda *_: (0,) * array.ndim)


def tiled(
    queries, keys, values, log_decay, residual, out_weight, gate_weight, up_weight, down_weight, expert_ids,
    route_weights, chunks, returns,
):
    seq_count, layers = lax.axis_size("seq"), lax.axis_size("mp")
    me, layer = lax.axis_index("seq"), lax.axis_index("mp")
    columns = seq_count // PAIR
    column = me // PAIR
    span, heads = queries.shape[0], log_decay.shape[0]
    size = queries.shape[1] // heads
    features = residual.shape[1]
    hidden_size = gate_weight.shape[2]
    tok = residual.shape[0]
    half = span // 2
    block = out_weight.shape[1]
    width = block // chunks
    chunk_width = seq_count * width
    capacity = max(2, tok * TOP * 3 // (2 * columns))
    slots = -(-layers * capacity // 16) * 16
    distances = [1 << i for i in range((layers - 1).bit_length())]
    order = [0]
    for d in reversed(distances):
        order = order + [b ^ d for b in order]

    away = [PAIR * (p % columns) + p // columns for p in range(seq_count)]
    blocks_at = jnp.stack([me ^ a for a in away]).astype(jnp.int32)
    rows_at = jnp.stack([layer ^ r for r in order]).astype(jnp.int32)

    def spread(array):
        own = [array] + [swap_columns(array, d) for d in range(1, columns)]
        return own + [swap_cores(a) for a in own]

    smem = pl.BlockSpec(memory_space=pltpu.SMEM)
    vmem = pl.BlockSpec(memory_space=pltpu.VMEM)

    def across(array):
        return [array] + [swap_columns(array, d) for d in range(1, columns)]

    def both_cores(arrays):
        return arrays + [swap_cores(a) for a in arrays]

    slices = [out_weight[:, i * width : (i + 1) * width] for i in range(chunks)]
    weights = [None] * chunks
    weights[0] = across(slices[0])
    state, local_part, weighted_queries = pl.pallas_call(
        local_kernel,
        out_shape=(
            jax.ShapeDtypeStruct((heads, size + DECAY_ROWS, size), BF16),
            jax.ShapeDtypeStruct((span, heads * size), F32),
            jax.ShapeDtypeStruct((span, heads * size), BF16),
        ),
        in_specs=[vmem] * 4,
        out_specs=(vmem,) * 3,
        compiler_params=params(),
        cost_estimate=cost(8 * heads * span * span * size, 1 << 20),
        name="local_attention",
    )(queries, keys, values, log_decay)
    states = across(state)

    flat = expert_ids.reshape(-1)
    count = flat.shape[0]
    before = jnp.arange(count)[:, None] > jnp.arange(count)[None, :]
    rank = jnp.sum((before & (flat[:, None] == flat[None, :])).astype(jnp.int32), axis=1).reshape(tok, TOP)
    route = jnp.concatenate(
        [expert_ids.astype(F32), rank.astype(F32), route_weights, jnp.zeros((tok, 2), F32)], axis=1
    )
    route = after(route, state)
    for d in reversed(distances):
        route = jnp.concatenate([route, swap_layers(route, d)], axis=0)
    ids, ranks = route[:, :TOP].astype(jnp.int32), route[:, TOP : 2 * TOP].astype(jnp.int32)
    gains = route[:, 2 * TOP : 3 * TOP]
    slot = (jnp.arange(span) // tok * capacity)[:, None] + ranks
    place = jnp.arange(columns * slots)
    target = jnp.where(ids[:, :, None] == (column ^ (place // slots))[None, None, :], slot[:, :, None], -1)
    hit = target == (place % slots)[None, None, :]
    pack_map = jnp.any(hit, axis=1).T.astype(BF16)
    mix = jnp.sum(jnp.where(hit, gains[:, :, None], 0.0), axis=1)
    mix_high = lax.reduce_precision(mix, 8, 7)
    mix_low = (mix - mix_high).astype(BF16)
    mix_high = mix_high.astype(BF16)

    near = after(residual, route)
    for d in reversed(distances[1:]):
        near = jnp.concatenate([near, swap_layers(near, d)], axis=0)

    weights[0] = both_cores(weights[0])
    weights[1] = across(after(slices[1], *states))
    states = both_cores(states)
    between = ((blocks_at[:, None] < blocks_at[None, :]) & (blocks_at[None, :] < me)).astype(F32)
    earlier = jnp.broadcast_to((blocks_at < me).astype(F32)[:, None], (seq_count, heads * size))
    normed = pl.pallas_call(
        functools.partial(prefix_kernel, seq_count, layers),
        out_shape=jax.ShapeDtypeStruct((span, heads * size), BF16),
        in_specs=[smem] + [vmem] * (4 + seq_count),
        out_specs=vmem,
        scratch_shapes=[pltpu.VMEM((seq_count, heads * size), F32), pltpu.VMEM((span, heads * size), BF16)],
        compiler_params=params(),
        cost_estimate=cost(2 * heads * span * size * size, 3 << 20),
        name="prefix_attention",
    )(rows_at, between, earlier, local_part, weighted_queries, *states)

    rows = 2 * columns * slots
    gate_view, up_view = gate_weight[0].T, up_weight[0].T

    def project(i, *earlier):
        keep, send = pl.pallas_call(
            functools.partial(project_kernel, seq_count),
            out_shape=(jax.ShapeDtypeStruct((half, chunk_width), BF16),) * 2,
            in_specs=[smem] + [vmem] * (1 + seq_count),
            out_specs=(vmem,) * 2,
            compiler_params=params(),
            cost_estimate=cost(2 * span * heads * size * chunk_width, 2 * heads * size * chunk_width),
            name="project",
        )(blocks_at, after(normed, *earlier), *weights[i])
        return keep, swap_layers(send, distances[0])

    def sum_layers(keep, arrived):
        part = (keep.astype(F32) + arrived.astype(F32)).astype(BF16)
        for d in distances[1:-1]:
            kept = part.shape[0] // 2
            part = (part[:kept].astype(F32) + swap_layers(part[kept:], d).astype(F32)).astype(BF16)
        return part, swap_layers(part, distances[-1])

    def add_residual(i, part, other):
        base = jnp.concatenate(
            [near[: 2 * tok, s * block + i * width : s * block + (i + 1) * width] for s in range(seq_count)], axis=1
        )
        other = jnp.concatenate([other[tok:], other[:tok]], axis=0)
        token = (base.astype(F32) + (part.astype(F32) + other.astype(F32))).astype(BF16)
        mine = token[:tok]
        for d in reversed(distances[1:-1]):
            token = jnp.concatenate([token, swap_layers(token, d)], axis=0)
        return mine, token, swap_layers(token, distances[0])

    def dispatch(token, far):
        tile = chunk_width // 4
        packed = pl.pallas_call(
            functools.partial(pack_kernel, columns),
            grid=(chunk_width // tile,),
            out_shape=(jax.ShapeDtypeStruct((slots, chunk_width), BF16),) * columns,
            in_specs=[
                whole_block(pack_map),
                pl.BlockSpec((half, tile), lambda n: (0, n)),
                pl.BlockSpec((half, tile), lambda n: (0, n)),
            ],
            out_specs=(pl.BlockSpec((slots, tile), lambda n: (0, n)),) * columns,
            compiler_params=params(),
            cost_estimate=cost(2 * columns * slots * span * chunk_width, 2 * columns * slots * chunk_width),
            name="pack",
        )(pack_map, token, far)
        return [packed[0]] + [swap_columns(packed[d], d) for d in range(1, columns)]

    steps = 2
    blocks = seq_count // steps
    sum_shapes = ((rows, 2 * hidden_size), (rows, 128))

    def gate_up(i, arrived, held):
        first, last = i == 0, i == chunks - 1

        def weight_block(b):
            return pl.BlockSpec((hidden_size, width), lambda s: (0, (s * blocks + b) * chunks + i))

        return pl.pallas_call(
            functools.partial(expert_kernel, seq_count, blocks, first, last, features),
            grid=(steps,),
            out_shape=jax.ShapeDtypeStruct((rows, hidden_size), BF16)
            if last
            else tuple(jax.ShapeDtypeStruct(s, F32) for s in sum_shapes),
            in_specs=[pl.BlockSpec((slots, blocks * width), lambda s: (0, s))] * seq_count
            + [weight_block(b) for b in range(blocks)] * 2
            + [whole_block(a) for a in held],
            out_specs=pl.BlockSpec((rows, hidden_size), lambda s: (0, 0))
            if last
            else tuple(pl.BlockSpec(s, lambda n: (0, 0)) for s in sum_shapes),
            scratch_shapes=[pltpu.VMEM(s, F32) for s in sum_shapes] if last else [],
            compiler_params=params(),
            cost_estimate=cost(4 * rows * hidden_size * chunk_width, 4 * hidden_size * chunk_width),
            name="gate_up",
        )(*arrived, *[gate_view] * blocks, *[up_view] * blocks, *held)

    projected, parts, tokens, arrived, sums = [None] * chunks, [None] * chunks, [None] * chunks, [None] * chunks, []
    projected[0] = project(0)
    for i in range(chunks):
        if i + 2 < chunks:
            weights[i + 2] = across(after(slices[i + 2], *weights[i + 1]))
        parts[i] = sum_layers(*projected[i])
        if i + 1 < chunks:
            weights[i + 1] = both_cores(weights[i + 1])
            projected[i + 1] = project(i + 1, projected[i][1])
        tokens[i] = add_residual(i, *parts[i])
        arrived[i] = dispatch(*tokens[i][1:])
    for i in range(chunks):
        sums = gate_up(i, both_cores(arrived[i]), sums)
    expert_hidden = sums

    own_hidden = jnp.concatenate(
        [tokens[i][0][:, s * width : (s + 1) * width] for s in range(seq_count) for i in range(chunks)], axis=1
    )
    out_width = features // returns
    tile = out_width // 4
    downs, backs, outputs = [None] * returns, [None] * returns, []

    def down(i):
        own, other = pl.pallas_call(
            down_kernel,
            grid=(out_width // tile,),
            out_shape=(jax.ShapeDtypeStruct((rows // 2, out_width), BF16),) * 2,
            in_specs=[
                whole_block(expert_hidden),
                pl.BlockSpec((hidden_size, tile), lambda n: (0, i * (out_width // tile) + n)),
            ],
            out_specs=(pl.BlockSpec((rows // 2, tile), lambda n: (0, n)),) * 2,
            compiler_params=params(),
            cost_estimate=cost(2 * rows * hidden_size * out_width, 4 * rows * out_width),
            name="down",
        )(expert_hidden, down_weight[0])
        return own, swap_cores(other)

    def send_back(own, other, *earlier):
        other = after(other, *earlier)
        summed = [
            (own[d * slots : (d + 1) * slots].astype(F32) + other[d * slots : (d + 1) * slots].astype(F32)).astype(BF16)
            for d in range(columns)
        ]
        return [summed[0]] + [swap_columns(summed[d], d) for d in range(1, columns)]

    def combine(back):
        keep, send = pl.pallas_call(
            functools.partial(combine_kernel, columns),
            grid=(out_width // tile,),
            out_shape=(
                jax.ShapeDtypeStruct((half, out_width), F32),
                jax.ShapeDtypeStruct((half, out_width), BF16),
            ),
            in_specs=[whole_block(mix_high), whole_block(mix_low)]
            + [pl.BlockSpec((slots, tile), lambda n: (0, n))] * columns,
            out_specs=(pl.BlockSpec((half, tile), lambda n: (0, n)),) * 2,
            compiler_params=params(),
            cost_estimate=cost(4 * span * columns * slots * out_width, 2 * columns * slots * out_width),
            name="combine",
        )(mix_high, mix_low, *back)
        return keep, swap_layers(send, distances[0])

    def finish(i, keep, arrived):
        part = keep + arrived.astype(F32)
        for d in distances[1:]:
            kept = part.shape[0] // 2
            part = part[:kept] + swap_layers(part[kept:].astype(BF16), d).astype(F32)
        mine = own_hidden[:, i * out_width : (i + 1) * out_width].astype(F32)
        return (mine + part).astype(BF16)

    downs = [down(i) for i in range(returns)]
    sent = []
    for i in range(returns):
        sent.append(send_back(*downs[i], *(sent[i - 1][1:3] if i else [])))
    for i in range(returns):
        outputs.append(finish(i, *combine(sent[i])))
    return jnp.concatenate(outputs, axis=1)


def general(
    queries,
    keys,
    values,
    log_decay,
    residual,
    out_weight,
    gate_weight,
    up_weight,
    down_weight,
    expert_ids,
    route_weights,
):
    seq_count = lax.axis_size("seq")
    span_len = queries.shape[0]
    head_count = log_decay.shape[0]
    head_size = queries.shape[1] // head_count
    query_heads = queries.reshape(span_len, head_count, head_size)
    key_heads = keys.reshape(span_len, head_count, head_size)
    value_heads = values.reshape(span_len, head_count, head_size)
    cumulative = jnp.cumsum(log_decay, axis=1)
    positions = jnp.arange(span_len)
    causal = (positions[:, None] >= positions[None, :])[None]
    spread_log = cumulative[:, :, None] - cumulative[:, None, :]
    weight = jnp.where(causal, jnp.exp(jnp.where(causal, spread_log, 0.0)), 0.0)
    raw_scores = jnp.einsum(
        "thd,shd->hts", query_heads, key_heads, preferred_element_type=jnp.float32
    )
    local_scores = (raw_scores * weight).astype(jnp.bfloat16)
    local_part = jnp.einsum(
        "hts,shd->thd", local_scores, value_heads, preferred_element_type=jnp.float32
    )
    span_total = cumulative[:, -1]
    key_scale = jnp.exp(span_total[:, None] - cumulative)
    weighted_keys = (key_scale.T[:, :, None] * key_heads.astype(jnp.float32)).astype(jnp.bfloat16)
    span_state = jnp.einsum(
        "thd,the->hde", weighted_keys, value_heads, preferred_element_type=jnp.float32
    ).astype(jnp.bfloat16)
    decays = lax.all_gather(span_total[None, :], "seq", axis=0, tiled=True)
    running = jnp.cumsum(decays, axis=0)
    my_index = lax.axis_index("seq")
    before = lax.dynamic_index_in_dim(running, jnp.maximum(my_index - 1, 0), 0, keepdims=False)
    shard_piece = lax.all_gather(span_state[None], "seq", axis=0, tiled=True)
    row_count = shard_piece.shape[0]
    source = jnp.arange(row_count)
    earlier_mask = (source < my_index)[:, None]
    factor = jnp.where(
        earlier_mask, jnp.exp(jnp.where(earlier_mask, before[None, :] - running, 0.0)), 0.0
    )
    prefix = jnp.einsum(
        "nh,nhde->hde", factor, shard_piece.astype(jnp.float32), precision=lax.Precision.HIGHEST
    )
    prefix_low = prefix.astype(jnp.bfloat16)
    weighted_queries = (jnp.exp(cumulative).T[:, :, None] * query_heads.astype(jnp.float32)).astype(
        jnp.bfloat16
    )
    carried_part = jnp.einsum(
        "thd,hde->the", weighted_queries, prefix_low, preferred_element_type=jnp.float32
    )
    mixed_heads = local_part + carried_part
    normed = (
        mixed_heads * lax.rsqrt(jnp.mean(mixed_heads * mixed_heads, axis=-1, keepdims=True) + 1e-06)
    ).astype(jnp.bfloat16)
    normed = normed.reshape(span_len, head_count * head_size)
    partial_out = jnp.dot(
        normed,
        lax.all_gather(out_weight, "seq", axis=1, tiled=True),
        preferred_element_type=jnp.float32,
    )
    attn_out = lax.psum_scatter(
        partial_out.astype(jnp.bfloat16), "mp", scatter_dimension=0, tiled=True
    ).astype(jnp.float32)
    hidden_state = (residual.astype(jnp.float32) + attn_out).astype(jnp.bfloat16)
    hidden_wide = hidden_state.astype(jnp.float32)
    moe_input = (
        hidden_wide * lax.rsqrt(jnp.mean(hidden_wide * hidden_wide, axis=-1, keepdims=True) + 1e-06)
    ).astype(jnp.bfloat16)
    model_width = residual.shape[1]
    experts = seq_count // PAIR
    tok_rows = residual.shape[0]
    capacity = max(2, tok_rows * TOP * 3 // (2 * experts))
    assign_count = tok_rows * TOP
    flat_ids = expert_ids.reshape(-1)
    expert_hot = (flat_ids[:, None] == jnp.arange(experts)[None, :]).astype(jnp.int32)
    slot_rank = jnp.sum((jnp.cumsum(expert_hot, axis=0) - expert_hot) * expert_hot, axis=1)
    target = flat_ids * capacity + slot_rank
    slot_hot = (target[:, None] == jnp.arange(experts * capacity)[None, :]).astype(jnp.float32)
    owner_hot = (
        (jnp.arange(assign_count) // TOP)[:, None] == jnp.arange(tok_rows)[None, :]
    ).astype(jnp.float32)
    dispatch_map = jnp.einsum("as,at->st", slot_hot, owner_hot).astype(jnp.bfloat16)
    packed = jnp.dot(dispatch_map, moe_input, preferred_element_type=jnp.float32).astype(
        jnp.bfloat16
    )
    outgoing = jnp.broadcast_to(
        packed.reshape(experts, 1, capacity, model_width), (experts, PAIR, capacity, model_width)
    )
    outgoing = outgoing.reshape(seq_count, capacity, model_width)
    incoming = lax.all_to_all(outgoing, "seq", split_axis=0, concat_axis=0, tiled=True)
    expert_rows = incoming.reshape(seq_count * capacity, model_width)
    gate_matrix = gate_weight[0]
    up_matrix = up_weight[0]
    down_matrix = down_weight[0]
    shard_piece = lax.all_gather(expert_rows, "mp", axis=0, tiled=True)
    gate_value = jnp.dot(shard_piece, gate_matrix, preferred_element_type=jnp.float32)
    lifted = jnp.dot(shard_piece, up_matrix, preferred_element_type=jnp.float32)
    hidden_rows = (jax.nn.silu(gate_value) * lifted).astype(jnp.bfloat16)
    half_out = lax.psum_scatter(
        jnp.dot(hidden_rows, down_matrix, preferred_element_type=jnp.float32).astype(jnp.bfloat16),
        "mp",
        scatter_dimension=0,
        tiled=True,
    )
    returned = lax.all_to_all(
        half_out.reshape(seq_count, capacity, model_width),
        "seq",
        split_axis=0,
        concat_axis=0,
        tiled=True,
    )
    expert_out = jnp.sum(
        returned.reshape(experts, PAIR, capacity, model_width).astype(jnp.float32), axis=1
    )
    expert_out = expert_out.reshape(experts * capacity, model_width)
    weighted = route_weights.reshape(-1)[:, None] * slot_hot
    combine_map = jnp.einsum("at,as->ts", owner_hot, weighted, precision=lax.Precision.HIGHEST)
    expert_mix = jnp.dot(combine_map, expert_out, precision=lax.Precision.HIGHEST)
    return (hidden_wide + expert_mix).astype(jnp.bfloat16)


def fits(mesh, tok, features, block, chunks, returns):
    layers, seq_count = mesh.shape["mp"], mesh.shape["seq"]
    powers = all(n & (n - 1) == 0 for n in (layers, seq_count)) and layers > 1 and seq_count > PAIR
    whole = block % (128 * chunks) == 0 and features % (512 * returns) == 0
    return powers and whole and tok % 16 == 0


def solution(mesh):
    placed = (
        P("seq", "mp"),
        P("seq", "mp"),
        P("seq", "mp"),
        P("mp", "seq"),
        P(("seq", "mp"), None),
        P("mp", "seq"),
        P("seq", None, "mp"),
        P("seq", None, "mp"),
        P("seq", "mp", None),
        P(("seq", "mp"), None),
        P(("seq", "mp"), None),
    )
    chunks, returns = 3, 3

    def per_device(*args):
        residual, out_weight = args[4], args[5]
        if fits(mesh, residual.shape[0], residual.shape[1], out_weight.shape[1], chunks, returns):
            return tiled(*args, chunks=chunks, returns=returns)
        return general(*args)

    return jax.shard_map(
        per_device, mesh=mesh, in_specs=placed, out_specs=P(("seq", "mp"), None), check_vma=False
    )
```

```python
import functools

import jax
import jax.numpy as jnp
from jax import lax
from jax.experimental import pallas as pl
from jax.experimental.pallas import tpu as pltpu
from jax.sharding import PartitionSpec as P

TOP = 2
PAIR = 2
VMEM_LIMIT = 44 * 1024 * 1024
EXTRA_ROWS = 16
ROUTE_ROWS = 10
HIGH = lax.Precision.HIGHEST
F32 = jnp.float32
BF16 = jnp.bfloat16


def params():
    return pltpu.CompilerParams(vmem_limit_bytes=VMEM_LIMIT)


def cost(microseconds):
    return pl.CostEstimate(flops=0, bytes_accessed=int(microseconds * 3.69e6), transcendentals=0)


def after(array, *earlier):
    return lax.optimization_barrier((array,) + earlier)[0]


def swap_columns(array, distance):
    count = lax.axis_size("seq")
    return lax.ppermute(array, "seq", [(i, i ^ (PAIR * distance)) for i in range(count)])


def swap_cores(array):
    count = lax.axis_size("seq")
    return lax.ppermute(array, "seq", [(i, i ^ 1) for i in range(count)])


def swap_layers(array, distance):
    count = lax.axis_size("mp")
    return lax.ppermute(array, "mp", [(i, i ^ distance) for i in range(count)])


def local_kernel(column_ref, q_ref, k_ref, v_ref, decay_ref, residual_ref, local_ref, weighted_ref, *message_refs):
    span = q_ref.shape[0]
    heads = decay_ref.shape[0]
    size = q_ref.shape[1] // heads
    row = lax.broadcasted_iota(jnp.int32, (span, span), 0)
    col = lax.broadcasted_iota(jnp.int32, (span, span), 1)
    causal = row >= col
    decay = decay_ref[...]
    along = jnp.dot(decay, (row <= col).astype(F32), precision=HIGH, preferred_element_type=F32)
    down = lax.dot_general(
        causal.astype(F32), decay, (((1,), (1,)), ((), ())), precision=HIGH, preferred_element_type=F32
    )
    extra = lax.broadcasted_iota(jnp.int32, (EXTRA_ROWS, size), 0)
    for h in range(heads):
        cols = slice(h * size, (h + 1) * size)
        q, k, v = q_ref[:, cols], k_ref[:, cols], v_ref[:, cols]
        here = down[:, h : h + 1]
        spread = here - along[h : h + 1, :]
        weight = jnp.where(causal, jnp.exp(jnp.where(causal, spread, 0.0)), 0.0)
        raw = lax.dot_general(q, k, (((1,), (1,)), ((), ())), preferred_element_type=F32)
        local_ref[:, cols] = jnp.dot((raw * weight).astype(BF16), v, preferred_element_type=F32)
        total = along[h : h + 1, span - 1 : span]
        scaled = (jnp.exp(total - here) * k.astype(F32)).astype(BF16)
        state = lax.dot_general(scaled, v, (((0,), (0,)), ((), ())), preferred_element_type=F32).astype(BF16)
        first = total.astype(BF16).astype(F32)
        second = (total - first).astype(BF16).astype(F32)
        third = total - first - second
        pieces = jnp.where(extra == 0, first, jnp.where(extra == 1, second, jnp.where(extra == 2, third, 0.0)))
        at = h * (size + EXTRA_ROWS)
        for message in message_refs:
            message[at : at + size, :] = state
            message[at + size : at + size + EXTRA_ROWS, :] = pieces.astype(BF16)
        weighted_ref[:, cols] = (jnp.exp(here) * q.astype(F32)).astype(BF16)
    tok = residual_ref.shape[0]
    first = heads * (size + EXTRA_ROWS)
    for d, message in enumerate(message_refs):
        parts = (message.shape[0] - first) // tok
        for b in range(parts):
            at = pl.multiple_of((column_ref[d] * parts + b) * size, size)
            message[first + b * tok : first + (b + 1) * tok, :] = residual_ref[:, pl.ds(at, size)]


def prefix_kernel(count, heads, layers, *refs):
    row_ref, between_ref, earlier_ref, local_ref, weighted_ref, route_ref = refs[:6]
    message_refs = refs[6 : 6 + count]
    out_ref, totals, held = refs[6 + count :]
    span = local_ref.shape[0]
    size = local_ref.shape[1] // heads
    tall = size + EXTRA_ROWS
    for p in range(count):
        for h in range(heads):
            extra = message_refs[p][h * tall + size : (h + 1) * tall, :].astype(F32)
            totals[p : p + 1, h * size : (h + 1) * size] = jnp.sum(extra, axis=0, keepdims=True)
    gap = jnp.dot(between_ref[...], totals[...], precision=HIGH, preferred_element_type=F32)
    totals[...] = jnp.exp(gap) * earlier_ref[...]
    for h in range(heads):
        cols = slice(h * size, (h + 1) * size)
        prefix = jnp.zeros((size, size), F32)
        for p in range(count):
            prefix += totals[p : p + 1, cols] * message_refs[p][h * tall : h * tall + size, :].astype(F32)
        mixed = local_ref[:, cols] + jnp.dot(
            weighted_ref[:, cols], prefix.astype(BF16), preferred_element_type=F32
        )
        mean = jnp.mean(mixed * mixed, axis=-1, keepdims=True)
        held[:, cols] = (mixed * lax.rsqrt(mean + 1e-06)).astype(BF16)
    rows = span // layers
    for r in range(layers):
        start = pl.multiple_of(row_ref[r] * rows, rows)
        out_ref[r * rows : (r + 1) * rows, :] = held[pl.ds(start, rows), :]
    out_ref[span:, :] = jnp.zeros((EXTRA_ROWS, heads * size), BF16)
    out_ref[span:, :span] = route_ref[...]


def map_kernel(count, columns, capacity, tok, column_ref, *refs):
    row_refs, (pack_ref, high_ref, low_ref) = refs[:count], refs[count:]
    slots, span = high_ref.shape[0] // columns, high_ref.shape[1]
    row = lax.broadcasted_iota(jnp.int32, (slots, span), 0)
    lane = lax.broadcasted_iota(jnp.int32, (1, span), 1)
    base = (lane // tok) * capacity
    for p in range(count):
        route = row_refs[p][span : span + EXTRA_ROWS, :span].astype(F32)
        for d in range(columns):
            expert = column_ref[d]
            hit, gain = None, None
            for k in range(TOP):
                named = route[k : k + 1].astype(jnp.int32) == expert
                rank = route[TOP + k : TOP + k + 1].astype(jnp.int32)
                at = 2 * TOP + 3 * k
                value = route[at : at + 1] + route[at + 1 : at + 2] + route[at + 2 : at + 3]
                here = jnp.where(named, base + rank, -1) == row
                weight = jnp.where(here, value, 0.0)
                hit = here if hit is None else hit | here
                gain = weight if gain is None else gain + weight
            pack_ref[p, d * slots : (d + 1) * slots, :] = jnp.where(hit, 1.0, 0.0).astype(BF16)
            if p == 0:
                high = gain.astype(BF16)
                high_ref[d * slots : (d + 1) * slots, :] = high
                low_ref[d * slots : (d + 1) * slots, :] = (gain - high.astype(F32)).astype(BF16)


def project_kernel(count, layers, tok, chunk, core_ref, *refs):
    row_refs, message_refs = refs[:count], refs[count : 2 * count]
    weight_ref, keep_ref, send_ref = refs[2 * count :]
    span = layers * tok
    rows = jnp.concatenate([ref[:span] for ref in row_refs], axis=0)
    part = jnp.dot(rows, weight_ref[...], preferred_element_type=F32).astype(BF16)
    lanes = message_refs[0].shape[1]
    pieces = weight_ref.shape[1] // lanes
    for r in range(layers):
        for p in range(count):
            to = (r % (layers // 2)) * count * tok + p * tok
            here = part[p * span + r * tok : p * span + (r + 1) * tok]
            if r >= layers // 2:
                send_ref[to : to + tok, :] = here
            elif r > 0:
                keep_ref[to : to + tok, :] = here.astype(F32)
            else:
                for b in range(pieces):
                    at = pl.multiple_of(core_ref[0] + (chunk * pieces + b) * tok, tok)
                    own = message_refs[p][pl.ds(at, tok), :].astype(F32)
                    cols = slice(b * lanes, (b + 1) * lanes)
                    keep_ref[to : to + tok, cols] = here[:, cols].astype(F32) + own


def pack_kernel(count, layers, place_ref, map_ref, near_ref, far_ref, *out_refs):
    slots = out_refs[0].shape[0] // count
    tok = near_ref.shape[0] // (layers // 2) // count
    for p in range(count):
        pieces = [
            ref[r * count * tok + p * tok : r * count * tok + (p + 1) * tok, :]
            for ref in (near_ref, far_ref)
            for r in range(layers // 2)
        ]
        tokens = jnp.concatenate(pieces, axis=0)
        packed = jnp.dot(map_ref[p], tokens, preferred_element_type=F32).astype(BF16)
        start = pl.multiple_of(place_ref[p] * slots, slots)
        for d in range(len(out_refs)):
            out_refs[d][pl.ds(start, slots), :] = packed[d * slots : (d + 1) * slots]


def expert_kernel(pieces, blocks, first, last, features, place_ref, *refs):
    x_refs = refs[:pieces]
    gate_refs, up_refs = refs[pieces : pieces + blocks], refs[pieces + blocks : pieces + 2 * blocks]
    rest = refs[pieces + 2 * blocks :]
    if not first:
        sum_in, square_in = rest[:2]
        rest = rest[2:]
    if last:
        out_ref, sum_ref, square_ref = rest
    else:
        sum_ref, square_ref = rest
    size = gate_refs[0].shape[0]
    even = size // 128 * 128
    lanes = square_ref.shape[1]
    step = pl.program_id(0)

    for s in range(pieces // blocks):

        @pl.when(step == s)
        def _(s=s):
            x = jnp.concatenate([ref[...] for ref in x_refs[s * blocks : (s + 1) * blocks]], axis=1)
            gate = jnp.concatenate([ref[...] for ref in gate_refs], axis=1)
            up = jnp.concatenate([ref[...] for ref in up_refs], axis=1)
            both = jnp.concatenate([gate[:even], up[:even], gate[even:], up[even:]], axis=0)
            sums = lax.dot_general(x, both, (((1,), (1,)), ((), ())), preferred_element_type=F32)
            wide = x.astype(F32)
            squares = wide[:, :lanes] * wide[:, :lanes]
            for i in range(1, x.shape[1] // lanes):
                part = wide[:, i * lanes : (i + 1) * lanes]
                squares += part * part
            if s > 0:
                sum_ref[...] += sums
                square_ref[...] += squares
            else:
                sum_ref[...] = sums if first else sum_in[...] + sums
                square_ref[...] = squares if first else square_in[...] + squares

    if last:

        @pl.when(step == pl.num_programs(0) - 1)
        def _():
            slots = out_ref.shape[0] // pieces

            def activate(gate, up, scale):
                gate = gate * scale
                return (gate / (1.0 + jnp.exp(-gate)) * (up * scale)).astype(BF16)

            for p in range(pieces):
                rows = pl.ds(pl.multiple_of(place_ref[p] * slots, slots), slots)
                to = slice(p * slots, (p + 1) * slots)
                mean = jnp.sum(square_ref[rows, :], axis=1, keepdims=True) / features
                scale = lax.rsqrt(mean + 1e-06)
                out_ref[to, :even] = activate(sum_ref[rows, :even], sum_ref[rows, even : 2 * even], scale)
                if even < size:
                    tail = sum_ref[rows, 2 * even :]
                    out_ref[to, even:] = activate(tail[:, : size - even], tail[:, size - even :], scale)


def down_kernel(hidden_ref, weight_ref, own_ref, *other_refs):
    half = own_ref.shape[0]
    out = jnp.dot(hidden_ref[...], weight_ref[...], preferred_element_type=F32).astype(BF16)
    own_ref[...] = out[:half]
    rows = half // len(other_refs)
    for d, ref in enumerate(other_refs):
        ref[...] = out[half + d * rows : half + (d + 1) * rows]


def combine_kernel(count, high_ref, low_ref, *refs):
    x_refs = refs[:count]
    keep_ref, send_ref = refs[count:]
    half = keep_ref.shape[0]
    x = jnp.concatenate([ref[...] for ref in x_refs], axis=0)
    out = lax.dot_general(high_ref[...], x, (((0,), (0,)), ((), ())), preferred_element_type=F32)
    out += lax.dot_general(low_ref[...], x, (((0,), (0,)), ((), ())), preferred_element_type=F32)
    keep_ref[...] = out[:half]
    send_ref[...] = out[half:].astype(BF16)


def whole_block(array):
    return pl.BlockSpec(array.shape, lambda *_: (0,) * array.ndim)


def tiled(
    queries, keys, values, log_decay, residual, out_weight, gate_weight, up_weight, down_weight, expert_ids,
    route_weights, chunks, returns,
):
    seq_count, layers = lax.axis_size("seq"), lax.axis_size("mp")
    me, layer = lax.axis_index("seq"), lax.axis_index("mp")
    columns = seq_count // PAIR
    column = me // PAIR
    span, heads = queries.shape[0], log_decay.shape[0]
    size = queries.shape[1] // heads
    features = residual.shape[1]
    hidden_size = gate_weight.shape[2]
    tok = residual.shape[0]
    half = span // 2
    block = out_weight.shape[1]
    width = block // chunks
    capacity = max(2, tok * TOP * 3 // (2 * columns))
    slots = layers * capacity
    distances = [1 << i for i in range((layers - 1).bit_length())]
    order = [0]
    for d in reversed(distances):
        order = order + [b ^ d for b in order]

    away = [PAIR * (p % columns) + p // columns for p in range(seq_count)]
    blocks_at = jnp.stack([me ^ a for a in away]).astype(jnp.int32)
    rows_at = jnp.stack([layer ^ r for r in order]).astype(jnp.int32)
    columns_at = jnp.stack([column ^ d for d in range(columns)]).astype(jnp.int32)

    def across(array):
        return [array] + [swap_columns(array, d) for d in range(1, columns)]

    def both_cores(arrays):
        arrays = list(arrays)
        return arrays + [swap_cores(a) for a in arrays]

    smem = pl.BlockSpec(memory_space=pltpu.SMEM)
    vmem = pl.BlockSpec(memory_space=pltpu.VMEM)
    residual_at = heads * (size + EXTRA_ROWS)
    message = (residual_at + PAIR * block // size * tok, size)
    local_part, weighted_queries, *messages = pl.pallas_call(
        local_kernel,
        out_shape=(
            jax.ShapeDtypeStruct((span, heads * size), F32),
            jax.ShapeDtypeStruct((span, heads * size), BF16),
        )
        + (jax.ShapeDtypeStruct(message, BF16),) * columns,
        grid=(1,),
        in_specs=[smem] + [whole_block(a) for a in (queries, keys, values, log_decay, residual)],
        out_specs=(pl.BlockSpec((span, heads * size), lambda n: (0, 0)),) * 2
        + (pl.BlockSpec(message, lambda n: (0, 0)),) * columns,
        compiler_params=params(),
        cost_estimate=cost(1.5),
        name="local_attention",
    )(columns_at, queries, keys, values, log_decay, residual)
    messages = [messages[0]] + [swap_columns(messages[d], d) for d in range(1, columns)]

    flat = after(expert_ids, local_part).reshape(-1)
    count = flat.shape[0]
    before = jnp.arange(count)[:, None] > jnp.arange(count)[None, :]
    rank = jnp.sum((before & (flat[:, None] == flat[None, :])).astype(jnp.int32), axis=1).reshape(tok, TOP)
    first = lax.reduce_precision(route_weights, 8, 7)
    second = lax.reduce_precision(route_weights - first, 8, 7)
    third = route_weights - first - second
    parts = jnp.stack([first, second, third], axis=2).reshape(tok, 3 * TOP)
    route = jnp.concatenate([expert_ids.astype(F32), rank.astype(F32), parts], axis=1).T.astype(BF16)
    route = jnp.pad(route, ((0, EXTRA_ROWS - ROUTE_ROWS), (0, 0)))
    for d in reversed(distances):
        route = jnp.concatenate([route, swap_layers(route, d)], axis=1)

    messages = both_cores([after(a, route) for a in messages])
    between = ((blocks_at[:, None] < blocks_at[None, :]) & (blocks_at[None, :] < me)).astype(F32)
    earlier = jnp.broadcast_to((blocks_at < me).astype(F32)[:, None], (seq_count, heads * size))
    normed = pl.pallas_call(
        functools.partial(prefix_kernel, seq_count, heads, layers),
        out_shape=jax.ShapeDtypeStruct((span + EXTRA_ROWS, heads * size), BF16),
        in_specs=[smem] + [vmem] * (5 + seq_count),
        out_specs=vmem,
        scratch_shapes=[pltpu.VMEM((seq_count, heads * size), F32), pltpu.VMEM((span, heads * size), BF16)],
        compiler_params=params(),
        cost_estimate=cost(1.2),
        name="prefix_attention",
    )(rows_at, between, earlier, local_part, weighted_queries, route, *messages)
    normed = both_cores(across(normed))

    core = me % PAIR
    core_at = (residual_at + core * (block // size * tok)).reshape(1).astype(jnp.int32)

    def slot_maps(*earlier):
        return pl.pallas_call(
            functools.partial(map_kernel, seq_count, columns, capacity, tok),
            out_shape=(
                jax.ShapeDtypeStruct((seq_count, columns * slots, span), BF16),
                jax.ShapeDtypeStruct((columns * slots, span), BF16),
                jax.ShapeDtypeStruct((columns * slots, span), BF16),
            ),
            in_specs=[smem] + [vmem] * seq_count,
            out_specs=(vmem,) * 3,
            compiler_params=params(),
            cost_estimate=cost(1.3),
            name="slot_maps",
        )(columns_at, after(normed[0], *earlier), *normed[1:])

    rows = seq_count * slots
    summed_rows = seq_count * half
    gate_view, up_view = gate_weight[0].T, up_weight[0].T

    def project(i, *earlier):
        keep, send = pl.pallas_call(
            functools.partial(project_kernel, seq_count, layers, tok, i),
            grid=(1,),
            out_shape=(
                jax.ShapeDtypeStruct((summed_rows, width), F32),
                jax.ShapeDtypeStruct((summed_rows, width), BF16),
            ),
            in_specs=[smem] + [whole_block(a) for a in (*normed, *messages)]
            + [pl.BlockSpec((heads * size, width), lambda n: (0, i))],
            out_specs=(pl.BlockSpec((summed_rows, width), lambda n: (0, 0)),) * 2,
            compiler_params=params(),
            cost_estimate=cost(1),
            name="project",
        )(core_at, after(normed[0], *earlier), *normed[1:], *messages, out_weight)
        return keep, swap_layers(send, distances[0])

    def sum_layers(keep, arrived):
        part = (keep + arrived.astype(F32)).astype(BF16)
        return part, swap_layers(part, distances[-1])

    def add_layers(part, other):
        middle = other.shape[0] // 2
        other = jnp.concatenate([other[middle:], other[:middle]], axis=0)
        token = (part.astype(F32) + other.astype(F32)).astype(BF16)
        return token, swap_layers(token, distances[0])

    def dispatch(token, far):
        packed = pl.pallas_call(
            functools.partial(pack_kernel, seq_count, layers),
            out_shape=(jax.ShapeDtypeStruct((rows, width), BF16),) * columns,
            in_specs=[smem] + [vmem] * 3,
            out_specs=(vmem,) * columns,
            compiler_params=params(),
            cost_estimate=cost(1),
            name="pack",
        )(blocks_at, pack_map, token, far)
        return [packed[0]] + [swap_columns(packed[d], d) for d in range(1, columns)]

    blocks = columns
    sum_shapes = ((rows, 2 * hidden_size), (rows, 128))

    def gate_up(i, arrived, held):
        first, last = i == 0, i == chunks - 1

        def weight_block(b):
            return pl.BlockSpec((hidden_size, width), lambda s, at: (0, at[s * blocks + b] * chunks + i))

        def constant(shape):
            return pl.BlockSpec(shape, lambda s, at: (0, 0))

        return pl.pallas_call(
            functools.partial(expert_kernel, seq_count, blocks, first, last, features),
            grid_spec=pltpu.PrefetchScalarGridSpec(
                num_scalar_prefetch=1,
                grid=(seq_count // blocks,),
                in_specs=[constant((rows, width))] * seq_count
                + [weight_block(b) for b in range(blocks)] * 2
                + [vmem] * len(held),
                out_specs=constant((rows, hidden_size)) if last else (vmem, vmem),
                scratch_shapes=[pltpu.VMEM(s, F32) for s in sum_shapes] if last else [],
            ),
            out_shape=jax.ShapeDtypeStruct((rows, hidden_size), BF16)
            if last
            else tuple(jax.ShapeDtypeStruct(s, F32) for s in sum_shapes),
            compiler_params=params(),
            cost_estimate=cost(24 / chunks),
            name="gate_up",
        )(blocks_at, *arrived, *[gate_view] * blocks, *[up_view] * blocks, *held)

    projected, sent, tokens, arrived, sums = [None] * chunks, [None] * chunks, [None] * chunks, [None] * chunks, []
    projected[0] = project(0)
    sent[0] = sum_layers(*projected[0])
    pack_map, mix_high, mix_low = slot_maps(sent[0][0])
    for i in range(chunks):
        if i + 1 < chunks:
            projected[i + 1] = project(i + 1, sent[i][0])
        if i == chunks - 1:
            both = both_cores(after(a, sent[i][0]) for a in arrived[0])
            sums = gate_up(0, both, sums)
            sent[i] = (after(sent[i][0], *sums), sent[i][1])
        tokens[i] = add_layers(*sent[i])
        if i + 1 < chunks:
            sent[i + 1] = sum_layers(*projected[i + 1])
        arrived[i] = dispatch(*tokens[i])
    for i in range(1, chunks):
        sums = gate_up(i, both_cores([after(a, *sums) for a in arrived[i]]), sums)

    middle = summed_rows // 2
    own = jnp.concatenate([token[:middle] for token, _ in tokens], axis=1)
    other = swap_cores(own[middle // 2 :])
    own = own[: middle // 2]
    joined = jnp.where(core == 0, jnp.concatenate([own, other], axis=1), jnp.concatenate([other, own], axis=1))
    expert_hidden = sums
    tile = 512

    def down(piece, *earlier):
        offset, out_width = piece
        own, *other = pl.pallas_call(
            down_kernel,
            grid=(out_width // tile,),
            out_shape=(jax.ShapeDtypeStruct((rows // 2, out_width), BF16),)
            + (jax.ShapeDtypeStruct((slots, out_width), BF16),) * columns,
            in_specs=[
                whole_block(expert_hidden),
                pl.BlockSpec((hidden_size, tile), lambda n: (0, offset // tile + n)),
            ],
            out_specs=(pl.BlockSpec((rows // 2, tile), lambda n: (0, n)),)
            + (pl.BlockSpec((slots, tile), lambda n: (0, n)),) * columns,
            compiler_params=params(),
            cost_estimate=cost(16 * out_width / features),
            name="down",
        )(after(expert_hidden, *earlier), down_weight[0])
        return own, [swap_cores(a) for a in other]

    def summed(own, other, *earlier):
        own = after(own, *earlier)
        return [
            (own[d * slots : (d + 1) * slots].astype(F32) + other[d].astype(F32)).astype(BF16)
            for d in range(columns)
        ]

    def combine(piece, back):
        out_width = piece[1]
        keep, send = pl.pallas_call(
            functools.partial(combine_kernel, columns),
            grid=(out_width // tile,),
            out_shape=(
                jax.ShapeDtypeStruct((half, out_width), F32),
                jax.ShapeDtypeStruct((half, out_width), BF16),
            ),
            in_specs=[whole_block(mix_high), whole_block(mix_low)]
            + [pl.BlockSpec((slots, tile), lambda n: (0, n))] * columns,
            out_specs=(pl.BlockSpec((half, tile), lambda n: (0, n)),) * 2,
            compiler_params=params(),
            cost_estimate=cost(1),
            name="combine",
        )(mix_high, mix_low, *back)
        return keep, swap_layers(send, distances[0])

    def layer_sum(keep, arrived):
        part = keep + arrived.astype(F32)
        kept = part.shape[0] // 2
        return part[:kept], swap_layers(part[kept:].astype(BF16), distances[-1])

    def finish(piece, part, arrived):
        mine = own_hidden[:, piece[0] : piece[0] + piece[1]].astype(F32)
        return (mine + (part + arrived.astype(F32))).astype(BF16)

    sent, mixed, last = [], [], []
    ahead = down(returns[0])
    joined = after(joined, ahead[0])
    joined = [joined[d * tok : (d + 1) * tok] for d in range(columns)]
    ahead = (after(ahead[0], *joined), ahead[1])
    joined = [joined[0]] + [swap_columns(joined[d], d) for d in range(1, columns)]
    for i, piece in enumerate(returns):
        earlier = sent[i - 1] + (joined if i == 1 else []) if i else []
        sums = summed(*ahead, *earlier)
        if i + 1 < len(returns):
            ahead = down(returns[i + 1], *sums)
        if i:
            mixed.append(combine(returns[i - 1], [after(a, *sums) for a in sent[i - 1]]))
        sent.append([sums[0]] + [swap_columns(sums[d], d) for d in range(1, columns)])
    earlier = []
    for i in range(len(returns) - 1):
        last.append(layer_sum(mixed[i][0], after(mixed[i][1], *earlier)))
        earlier = [last[i][1]] if i + 2 < len(returns) else [last[i][0]]
    mixed.append(combine(returns[-1], [after(a, *earlier) for a in sent[-1]]))
    last.append(layer_sum(*mixed[-1]))

    joined = jnp.concatenate(joined, axis=0)
    own_hidden = jnp.concatenate(
        [lax.dynamic_slice_in_dim(joined, columns_at[d] * tok, tok, 0) for d in range(columns)], axis=1
    )
    outputs = [finish(piece, *last[i]) for i, piece in enumerate(returns)]
    return jnp.concatenate(outputs, axis=1)


def general(
    queries,
    keys,
    values,
    log_decay,
    residual,
    out_weight,
    gate_weight,
    up_weight,
    down_weight,
    expert_ids,
    route_weights,
):
    seq_count = lax.axis_size("seq")
    span_len = queries.shape[0]
    head_count = log_decay.shape[0]
    head_size = queries.shape[1] // head_count
    query_heads = queries.reshape(span_len, head_count, head_size)
    key_heads = keys.reshape(span_len, head_count, head_size)
    value_heads = values.reshape(span_len, head_count, head_size)
    cumulative = jnp.cumsum(log_decay, axis=1)
    positions = jnp.arange(span_len)
    causal = (positions[:, None] >= positions[None, :])[None]
    spread_log = cumulative[:, :, None] - cumulative[:, None, :]
    weight = jnp.where(causal, jnp.exp(jnp.where(causal, spread_log, 0.0)), 0.0)
    raw_scores = jnp.einsum(
        "thd,shd->hts", query_heads, key_heads, preferred_element_type=jnp.float32
    )
    local_scores = (raw_scores * weight).astype(jnp.bfloat16)
    local_part = jnp.einsum(
        "hts,shd->thd", local_scores, value_heads, preferred_element_type=jnp.float32
    )
    span_total = cumulative[:, -1]
    key_scale = jnp.exp(span_total[:, None] - cumulative)
    weighted_keys = (key_scale.T[:, :, None] * key_heads.astype(jnp.float32)).astype(jnp.bfloat16)
    span_state = jnp.einsum(
        "thd,the->hde", weighted_keys, value_heads, preferred_element_type=jnp.float32
    ).astype(jnp.bfloat16)
    decays = lax.all_gather(span_total[None, :], "seq", axis=0, tiled=True)
    running = jnp.cumsum(decays, axis=0)
    my_index = lax.axis_index("seq")
    before = lax.dynamic_index_in_dim(running, jnp.maximum(my_index - 1, 0), 0, keepdims=False)
    shard_piece = lax.all_gather(span_state[None], "seq", axis=0, tiled=True)
    row_count = shard_piece.shape[0]
    source = jnp.arange(row_count)
    earlier_mask = (source < my_index)[:, None]
    factor = jnp.where(
        earlier_mask, jnp.exp(jnp.where(earlier_mask, before[None, :] - running, 0.0)), 0.0
    )
    prefix = jnp.einsum(
        "nh,nhde->hde", factor, shard_piece.astype(jnp.float32), precision=lax.Precision.HIGHEST
    )
    prefix_low = prefix.astype(jnp.bfloat16)
    weighted_queries = (jnp.exp(cumulative).T[:, :, None] * query_heads.astype(jnp.float32)).astype(
        jnp.bfloat16
    )
    carried_part = jnp.einsum(
        "thd,hde->the", weighted_queries, prefix_low, preferred_element_type=jnp.float32
    )
    mixed_heads = local_part + carried_part
    normed = (
        mixed_heads * lax.rsqrt(jnp.mean(mixed_heads * mixed_heads, axis=-1, keepdims=True) + 1e-06)
    ).astype(jnp.bfloat16)
    normed = normed.reshape(span_len, head_count * head_size)
    partial_out = jnp.dot(
        normed,
        lax.all_gather(out_weight, "seq", axis=1, tiled=True),
        preferred_element_type=jnp.float32,
    )
    attn_out = lax.psum_scatter(
        partial_out.astype(jnp.bfloat16), "mp", scatter_dimension=0, tiled=True
    ).astype(jnp.float32)
    hidden_state = (residual.astype(jnp.float32) + attn_out).astype(jnp.bfloat16)
    hidden_wide = hidden_state.astype(jnp.float32)
    moe_input = (
        hidden_wide * lax.rsqrt(jnp.mean(hidden_wide * hidden_wide, axis=-1, keepdims=True) + 1e-06)
    ).astype(jnp.bfloat16)
    model_width = residual.shape[1]
    experts = seq_count // PAIR
    tok_rows = residual.shape[0]
    capacity = max(2, tok_rows * TOP * 3 // (2 * experts))
    assign_count = tok_rows * TOP
    flat_ids = expert_ids.reshape(-1)
    expert_hot = (flat_ids[:, None] == jnp.arange(experts)[None, :]).astype(jnp.int32)
    slot_rank = jnp.sum((jnp.cumsum(expert_hot, axis=0) - expert_hot) * expert_hot, axis=1)
    target = flat_ids * capacity + slot_rank
    slot_hot = (target[:, None] == jnp.arange(experts * capacity)[None, :]).astype(jnp.float32)
    owner_hot = (
        (jnp.arange(assign_count) // TOP)[:, None] == jnp.arange(tok_rows)[None, :]
    ).astype(jnp.float32)
    dispatch_map = jnp.einsum("as,at->st", slot_hot, owner_hot).astype(jnp.bfloat16)
    packed = jnp.dot(dispatch_map, moe_input, preferred_element_type=jnp.float32).astype(
        jnp.bfloat16
    )
    outgoing = jnp.broadcast_to(
        packed.reshape(experts, 1, capacity, model_width), (experts, PAIR, capacity, model_width)
    )
    outgoing = outgoing.reshape(seq_count, capacity, model_width)
    incoming = lax.all_to_all(outgoing, "seq", split_axis=0, concat_axis=0, tiled=True)
    expert_rows = incoming.reshape(seq_count * capacity, model_width)
    gate_matrix = gate_weight[0]
    up_matrix = up_weight[0]
    down_matrix = down_weight[0]
    shard_piece = lax.all_gather(expert_rows, "mp", axis=0, tiled=True)
    gate_value = jnp.dot(shard_piece, gate_matrix, preferred_element_type=jnp.float32)
    lifted = jnp.dot(shard_piece, up_matrix, preferred_element_type=jnp.float32)
    hidden_rows = (jax.nn.silu(gate_value) * lifted).astype(jnp.bfloat16)
    half_out = lax.psum_scatter(
        jnp.dot(hidden_rows, down_matrix, preferred_element_type=jnp.float32).astype(jnp.bfloat16),
        "mp",
        scatter_dimension=0,
        tiled=True,
    )
    returned = lax.all_to_all(
        half_out.reshape(seq_count, capacity, model_width),
        "seq",
        split_axis=0,
        concat_axis=0,
        tiled=True,
    )
    expert_out = jnp.sum(
        returned.reshape(experts, PAIR, capacity, model_width).astype(jnp.float32), axis=1
    )
    expert_out = expert_out.reshape(experts * capacity, model_width)
    weighted = route_weights.reshape(-1)[:, None] * slot_hot
    combine_map = jnp.einsum("at,as->ts", owner_hot, weighted, precision=lax.Precision.HIGHEST)
    expert_mix = jnp.dot(combine_map, expert_out, precision=lax.Precision.HIGHEST)
    return (hidden_wide + expert_mix).astype(jnp.bfloat16)


def cuts(tile, parts):
    return [(sum(parts[:i]) * tile, part * tile) for i, part in enumerate(parts)]


def fits(mesh, tok, features, block, chunks):
    layers, seq_count = mesh.shape["mp"], mesh.shape["seq"]
    powers = seq_count & (seq_count - 1) == 0 and seq_count > PAIR
    return powers and layers == 4 and tok % 16 == 0 and block % (128 * chunks) == 0 and features % (512 * 12) == 0


def solution(mesh):
    placed = (
        P("seq", "mp"),
        P("seq", "mp"),
        P("seq", "mp"),
        P("mp", "seq"),
        P(("seq", "mp"), None),
        P("mp", "seq"),
        P("seq", None, "mp"),
        P("seq", None, "mp"),
        P("seq", "mp", None),
        P(("seq", "mp"), None),
        P(("seq", "mp"), None),
    )
    chunks = 3

    def per_device(*args):
        residual, out_weight = args[4], args[5]
        features, block = residual.shape[1], out_weight.shape[1]
        if fits(mesh, residual.shape[0], features, block, chunks):
            return tiled(*args, chunks=chunks, returns=cuts(features // 12, [2, 4, 4, 2]))
        return general(*args)

    return jax.shard_map(
        per_device, mesh=mesh, in_specs=placed, out_specs=P(("seq", "mp"), None), check_vma=False
    )
```

```python
import functools

import jax
import jax.numpy as jnp
from jax import lax
from jax.experimental import pallas as pl
from jax.experimental.pallas import tpu as pltpu
from jax.sharding import PartitionSpec as P

TOP = 2
PAIR = 2
VMEM_LIMIT = 44 * 1024 * 1024
EXTRA_ROWS = 16
ROUTE_ROWS = 10
HIGH = lax.Precision.HIGHEST
F32 = jnp.float32
BF16 = jnp.bfloat16


def params():
    return pltpu.CompilerParams(vmem_limit_bytes=VMEM_LIMIT)


def cost(microseconds):
    return pl.CostEstimate(flops=0, bytes_accessed=int(microseconds * 3.69e6), transcendentals=0)


def after(array, *earlier):
    return lax.optimization_barrier((array,) + earlier)[0]


def swap_columns(array, distance):
    count = lax.axis_size("seq")
    return lax.ppermute(array, "seq", [(i, i ^ (PAIR * distance)) for i in range(count)])


def swap_cores(array):
    count = lax.axis_size("seq")
    return lax.ppermute(array, "seq", [(i, i ^ 1) for i in range(count)])


def swap_layers(array, distance):
    count = lax.axis_size("mp")
    return lax.ppermute(array, "mp", [(i, i ^ distance) for i in range(count)])


def local_kernel(column_ref, q_ref, k_ref, v_ref, decay_ref, residual_ref, local_ref, weighted_ref, *message_refs):
    span = q_ref.shape[0]
    heads = decay_ref.shape[0]
    size = q_ref.shape[1] // heads
    row = lax.broadcasted_iota(jnp.int32, (span, span), 0)
    col = lax.broadcasted_iota(jnp.int32, (span, span), 1)
    causal = row >= col
    decay = decay_ref[...]
    along = jnp.dot(decay, (row <= col).astype(F32), precision=HIGH, preferred_element_type=F32)
    down = lax.dot_general(
        causal.astype(F32), decay, (((1,), (1,)), ((), ())), precision=HIGH, preferred_element_type=F32
    )
    extra = lax.broadcasted_iota(jnp.int32, (EXTRA_ROWS, size), 0)
    for h in range(heads):
        cols = slice(h * size, (h + 1) * size)
        q, k, v = q_ref[:, cols], k_ref[:, cols], v_ref[:, cols]
        here = down[:, h : h + 1]
        spread = here - along[h : h + 1, :]
        weight = jnp.where(causal, jnp.exp(jnp.where(causal, spread, 0.0)), 0.0)
        raw = lax.dot_general(q, k, (((1,), (1,)), ((), ())), preferred_element_type=F32)
        local_ref[:, cols] = jnp.dot((raw * weight).astype(BF16), v, preferred_element_type=F32)
        total = along[h : h + 1, span - 1 : span]
        scaled = (jnp.exp(total - here) * k.astype(F32)).astype(BF16)
        state = lax.dot_general(scaled, v, (((0,), (0,)), ((), ())), preferred_element_type=F32).astype(BF16)
        first = total.astype(BF16).astype(F32)
        second = (total - first).astype(BF16).astype(F32)
        third = total - first - second
        pieces = jnp.where(extra == 0, first, jnp.where(extra == 1, second, jnp.where(extra == 2, third, 0.0)))
        at = h * (size + EXTRA_ROWS)
        for message in message_refs:
            message[at : at + size, :] = state
            message[at + size : at + size + EXTRA_ROWS, :] = pieces.astype(BF16)
        weighted_ref[:, cols] = (jnp.exp(here) * q.astype(F32)).astype(BF16)
    tok = residual_ref.shape[0]
    first = heads * (size + EXTRA_ROWS)
    for d, message in enumerate(message_refs):
        parts = (message.shape[0] - first) // tok
        for b in range(parts):
            at = pl.multiple_of((column_ref[d] * parts + b) * size, size)
            message[first + b * tok : first + (b + 1) * tok, :] = residual_ref[:, pl.ds(at, size)]


def prefix_kernel(count, heads, layers, *refs):
    row_ref, between_ref, earlier_ref, local_ref, weighted_ref, route_ref = refs[:6]
    message_refs = refs[6 : 6 + count]
    out_ref, totals, held = refs[6 + count :]
    span = local_ref.shape[0]
    size = local_ref.shape[1] // heads
    tall = size + EXTRA_ROWS
    for p in range(count):
        for h in range(heads):
            extra = message_refs[p][h * tall + size : (h + 1) * tall, :].astype(F32)
            totals[p : p + 1, h * size : (h + 1) * size] = jnp.sum(extra, axis=0, keepdims=True)
    gap = jnp.dot(between_ref[...], totals[...], precision=HIGH, preferred_element_type=F32)
    totals[...] = jnp.exp(gap) * earlier_ref[...]
    for h in range(heads):
        cols = slice(h * size, (h + 1) * size)
        prefix = jnp.zeros((size, size), F32)
        for p in range(count):
            prefix += totals[p : p + 1, cols] * message_refs[p][h * tall : h * tall + size, :].astype(F32)
        mixed = local_ref[:, cols] + jnp.dot(
            weighted_ref[:, cols], prefix.astype(BF16), preferred_element_type=F32
        )
        mean = jnp.mean(mixed * mixed, axis=-1, keepdims=True)
        held[:, cols] = (mixed * lax.rsqrt(mean + 1e-06)).astype(BF16)
    rows = span // layers
    for r in range(layers):
        start = pl.multiple_of(row_ref[r] * rows, rows)
        out_ref[r * rows : (r + 1) * rows, :] = held[pl.ds(start, rows), :]
    out_ref[span:, :] = jnp.zeros((EXTRA_ROWS, heads * size), BF16)
    out_ref[span:, :span] = route_ref[...]


def map_kernel(count, columns, capacity, tok, column_ref, *refs):
    row_refs, (pack_ref, high_ref, low_ref) = refs[:count], refs[count:]
    slots, span = high_ref.shape[0] // columns, high_ref.shape[1]
    row = lax.broadcasted_iota(jnp.int32, (slots, span), 0)
    lane = lax.broadcasted_iota(jnp.int32, (1, span), 1)
    base = (lane // tok) * capacity
    for p in range(count):
        route = row_refs[p][span : span + EXTRA_ROWS, :span].astype(F32)
        for d in range(columns):
            expert = column_ref[d]
            hit, gain = None, None
            for k in range(TOP):
                named = route[k : k + 1].astype(jnp.int32) == expert
                rank = route[TOP + k : TOP + k + 1].astype(jnp.int32)
                at = 2 * TOP + 3 * k
                value = route[at : at + 1] + route[at + 1 : at + 2] + route[at + 2 : at + 3]
                here = jnp.where(named, base + rank, -1) == row
                weight = jnp.where(here, value, 0.0)
                hit = here if hit is None else hit | here
                gain = weight if gain is None else gain + weight
            pack_ref[p, d * slots : (d + 1) * slots, :] = jnp.where(hit, 1.0, 0.0).astype(BF16)
            if p == 0:
                high = gain.astype(BF16)
                high_ref[d * slots : (d + 1) * slots, :] = high
                low_ref[d * slots : (d + 1) * slots, :] = (gain - high.astype(F32)).astype(BF16)


def project_kernel(count, layers, tok, chunk, core_ref, *refs):
    row_refs, message_refs = refs[:count], refs[count : 2 * count]
    weight_ref, keep_ref, send_ref = refs[2 * count :]
    span = layers * tok
    rows = jnp.concatenate([ref[:span] for ref in row_refs], axis=0)
    part = jnp.dot(rows, weight_ref[...], preferred_element_type=F32).astype(BF16)
    lanes = message_refs[0].shape[1]
    pieces = weight_ref.shape[1] // lanes
    for r in range(layers):
        for p in range(count):
            to = (r % (layers // 2)) * count * tok + p * tok
            here = part[p * span + r * tok : p * span + (r + 1) * tok]
            if r >= layers // 2:
                send_ref[to : to + tok, :] = here
            elif r > 0:
                keep_ref[to : to + tok, :] = here.astype(F32)
            else:
                for b in range(pieces):
                    at = pl.multiple_of(core_ref[0] + (chunk * pieces + b) * tok, tok)
                    own = message_refs[p][pl.ds(at, tok), :].astype(F32)
                    cols = slice(b * lanes, (b + 1) * lanes)
                    keep_ref[to : to + tok, cols] = here[:, cols].astype(F32) + own


def pack_kernel(count, layers, place_ref, map_ref, near_ref, far_ref, *out_refs):
    slots = out_refs[0].shape[0] // count
    tok = near_ref.shape[0] // (layers // 2) // count
    for p in range(count):
        pieces = [
            ref[r * count * tok + p * tok : r * count * tok + (p + 1) * tok, :]
            for ref in (near_ref, far_ref)
            for r in range(layers // 2)
        ]
        tokens = jnp.concatenate(pieces, axis=0)
        packed = jnp.dot(map_ref[p], tokens, preferred_element_type=F32).astype(BF16)
        start = pl.multiple_of(place_ref[p] * slots, slots)
        for d in range(len(out_refs)):
            out_refs[d][pl.ds(start, slots), :] = packed[d * slots : (d + 1) * slots]


def expert_kernel(pieces, blocks, first, last, features, place_ref, *refs):
    x_refs = refs[:pieces]
    gate_refs, up_refs = refs[pieces : pieces + blocks], refs[pieces + blocks : pieces + 2 * blocks]
    rest = refs[pieces + 2 * blocks :]
    if not first:
        sum_in, square_in = rest[:2]
        rest = rest[2:]
    if last:
        out_ref, sum_ref, square_ref = rest
    else:
        sum_ref, square_ref = rest
    size = gate_refs[0].shape[0]
    even = size // 128 * 128
    lanes = square_ref.shape[1]
    step = pl.program_id(0)

    for s in range(pieces // blocks):

        @pl.when(step == s)
        def _(s=s):
            x = jnp.concatenate([ref[...] for ref in x_refs[s * blocks : (s + 1) * blocks]], axis=1)
            gate = jnp.concatenate([ref[...] for ref in gate_refs], axis=1)
            up = jnp.concatenate([ref[...] for ref in up_refs], axis=1)
            both = jnp.concatenate([gate[:even], up[:even], gate[even:], up[even:]], axis=0)
            sums = lax.dot_general(x, both, (((1,), (1,)), ((), ())), preferred_element_type=F32)
            wide = x.astype(F32)
            squares = wide[:, :lanes] * wide[:, :lanes]
            for i in range(1, x.shape[1] // lanes):
                part = wide[:, i * lanes : (i + 1) * lanes]
                squares += part * part
            if s > 0:
                sum_ref[...] += sums
                square_ref[...] += squares
            else:
                sum_ref[...] = sums if first else sum_in[...] + sums
                square_ref[...] = squares if first else square_in[...] + squares

    if last:

        @pl.when(step == pl.num_programs(0) - 1)
        def _():
            slots = out_ref.shape[0] // pieces

            def activate(gate, up, scale):
                gate = gate * scale
                return (gate / (1.0 + jnp.exp(-gate)) * (up * scale)).astype(BF16)

            for p in range(pieces):
                rows = pl.ds(pl.multiple_of(place_ref[p] * slots, slots), slots)
                to = slice(p * slots, (p + 1) * slots)
                mean = jnp.sum(square_ref[rows, :], axis=1, keepdims=True) / features
                scale = lax.rsqrt(mean + 1e-06)
                out_ref[to, :even] = activate(sum_ref[rows, :even], sum_ref[rows, even : 2 * even], scale)
                if even < size:
                    tail = sum_ref[rows, 2 * even :]
                    out_ref[to, even:] = activate(tail[:, : size - even], tail[:, size - even :], scale)


def down_kernel(hidden_ref, weight_ref, own_ref, *other_refs):
    half = own_ref.shape[0]
    out = jnp.dot(hidden_ref[...], weight_ref[...], preferred_element_type=F32).astype(BF16)
    own_ref[...] = out[:half]
    rows = half // len(other_refs)
    for d, ref in enumerate(other_refs):
        ref[...] = out[half + d * rows : half + (d + 1) * rows]


def combine_kernel(count, high_ref, low_ref, *refs):
    x_refs = refs[:count]
    keep_ref, send_ref = refs[count:]
    half = keep_ref.shape[0]
    x = jnp.concatenate([ref[...] for ref in x_refs], axis=0)
    out = lax.dot_general(high_ref[...], x, (((0,), (0,)), ((), ())), preferred_element_type=F32)
    out += lax.dot_general(low_ref[...], x, (((0,), (0,)), ((), ())), preferred_element_type=F32)
    keep_ref[...] = out[:half]
    send_ref[...] = out[half:].astype(BF16)


def whole_block(array):
    return pl.BlockSpec(array.shape, lambda *_: (0,) * array.ndim)


def tiled(
    queries, keys, values, log_decay, residual, out_weight, gate_weight, up_weight, down_weight, expert_ids,
    route_weights, chunks, returns,
):
    seq_count, layers = lax.axis_size("seq"), lax.axis_size("mp")
    me, layer = lax.axis_index("seq"), lax.axis_index("mp")
    columns = seq_count // PAIR
    column = me // PAIR
    span, heads = queries.shape[0], log_decay.shape[0]
    size = queries.shape[1] // heads
    features = residual.shape[1]
    hidden_size = gate_weight.shape[2]
    tok = residual.shape[0]
    half = span // 2
    block = out_weight.shape[1]
    width = block // chunks
    capacity = max(2, tok * TOP * 3 // (2 * columns))
    slots = layers * capacity
    distances = [1 << i for i in range((layers - 1).bit_length())]
    order = [0]
    for d in reversed(distances):
        order = order + [b ^ d for b in order]

    away = [PAIR * (p % columns) + p // columns for p in range(seq_count)]
    blocks_at = jnp.stack([me ^ a for a in away]).astype(jnp.int32)
    rows_at = jnp.stack([layer ^ r for r in order]).astype(jnp.int32)
    columns_at = jnp.stack([column ^ d for d in range(columns)]).astype(jnp.int32)

    def across(array):
        return [array] + [swap_columns(array, d) for d in range(1, columns)]

    def both_cores(arrays):
        arrays = list(arrays)
        return arrays + [swap_cores(a) for a in arrays]

    smem = pl.BlockSpec(memory_space=pltpu.SMEM)
    vmem = pl.BlockSpec(memory_space=pltpu.VMEM)
    residual_at = heads * (size + EXTRA_ROWS)
    message = (residual_at + PAIR * block // size * tok, size)
    local_part, weighted_queries, *messages = pl.pallas_call(
        local_kernel,
        out_shape=(
            jax.ShapeDtypeStruct((span, heads * size), F32),
            jax.ShapeDtypeStruct((span, heads * size), BF16),
        )
        + (jax.ShapeDtypeStruct(message, BF16),) * columns,
        grid=(1,),
        in_specs=[smem] + [whole_block(a) for a in (queries, keys, values, log_decay, residual)],
        out_specs=(pl.BlockSpec((span, heads * size), lambda n: (0, 0)),) * 2
        + (pl.BlockSpec(message, lambda n: (0, 0)),) * columns,
        compiler_params=params(),
        cost_estimate=cost(1.5),
        name="local_attention",
    )(columns_at, queries, keys, values, log_decay, residual)
    messages = [messages[0]] + [swap_columns(messages[d], d) for d in range(1, columns)]

    flat = after(expert_ids, local_part).reshape(-1)
    count = flat.shape[0]
    before = jnp.arange(count)[:, None] > jnp.arange(count)[None, :]
    rank = jnp.sum((before & (flat[:, None] == flat[None, :])).astype(jnp.int32), axis=1).reshape(tok, TOP)
    first = lax.reduce_precision(route_weights, 8, 7)
    second = lax.reduce_precision(route_weights - first, 8, 7)
    third = route_weights - first - second
    parts = jnp.stack([first, second, third], axis=2).reshape(tok, 3 * TOP)
    route = jnp.concatenate([expert_ids.astype(F32), rank.astype(F32), parts], axis=1).T.astype(BF16)
    route = jnp.pad(route, ((0, EXTRA_ROWS - ROUTE_ROWS), (0, 0)))
    for d in reversed(distances):
        route = jnp.concatenate([route, swap_layers(route, d)], axis=1)

    messages = both_cores([after(a, route) for a in messages])
    between = ((blocks_at[:, None] < blocks_at[None, :]) & (blocks_at[None, :] < me)).astype(F32)
    earlier = jnp.broadcast_to((blocks_at < me).astype(F32)[:, None], (seq_count, heads * size))
    normed = pl.pallas_call(
        functools.partial(prefix_kernel, seq_count, heads, layers),
        out_shape=jax.ShapeDtypeStruct((span + EXTRA_ROWS, heads * size), BF16),
        in_specs=[smem] + [vmem] * (5 + seq_count),
        out_specs=vmem,
        scratch_shapes=[pltpu.VMEM((seq_count, heads * size), F32), pltpu.VMEM((span, heads * size), BF16)],
        compiler_params=params(),
        cost_estimate=cost(1.2),
        name="prefix_attention",
    )(rows_at, between, earlier, local_part, weighted_queries, route, *messages)
    normed = both_cores(across(normed))

    core = me % PAIR
    core_at = (residual_at + core * (block // size * tok)).reshape(1).astype(jnp.int32)

    def slot_maps(*earlier):
        return pl.pallas_call(
            functools.partial(map_kernel, seq_count, columns, capacity, tok),
            out_shape=(
                jax.ShapeDtypeStruct((seq_count, columns * slots, span), BF16),
                jax.ShapeDtypeStruct((columns * slots, span), BF16),
                jax.ShapeDtypeStruct((columns * slots, span), BF16),
            ),
            in_specs=[smem] + [vmem] * seq_count,
            out_specs=(vmem,) * 3,
            compiler_params=params(),
            cost_estimate=cost(1.3),
            name="slot_maps",
        )(columns_at, after(normed[0], *earlier), *normed[1:])

    rows = seq_count * slots
    summed_rows = seq_count * half
    gate_view, up_view = gate_weight[0].T, up_weight[0].T

    def project(i, *earlier):
        keep, send = pl.pallas_call(
            functools.partial(project_kernel, seq_count, layers, tok, i),
            grid=(1,),
            out_shape=(
                jax.ShapeDtypeStruct((summed_rows, width), F32),
                jax.ShapeDtypeStruct((summed_rows, width), BF16),
            ),
            in_specs=[smem] + [whole_block(a) for a in (*normed, *messages)]
            + [pl.BlockSpec((heads * size, width), lambda n: (0, i))],
            out_specs=(pl.BlockSpec((summed_rows, width), lambda n: (0, 0)),) * 2,
            compiler_params=params(),
            cost_estimate=cost(1),
            name="project",
        )(core_at, after(normed[0], *earlier), *normed[1:], *messages, out_weight)
        return keep, swap_layers(send, distances[0])

    def sum_layers(keep, arrived):
        part = (keep + arrived.astype(F32)).astype(BF16)
        return part, swap_layers(part, distances[-1])

    def add_layers(part, other):
        middle = other.shape[0] // 2
        other = jnp.concatenate([other[middle:], other[:middle]], axis=0)
        token = (part.astype(F32) + other.astype(F32)).astype(BF16)
        return token, swap_layers(token, distances[0])

    def dispatch(token, far):
        packed = pl.pallas_call(
            functools.partial(pack_kernel, seq_count, layers),
            out_shape=(jax.ShapeDtypeStruct((rows, width), BF16),) * columns,
            in_specs=[smem] + [vmem] * 3,
            out_specs=(vmem,) * columns,
            compiler_params=params(),
            cost_estimate=cost(1),
            name="pack",
        )(blocks_at, pack_map, token, far)
        return [packed[0]] + [swap_columns(packed[d], d) for d in range(1, columns)]

    blocks = columns
    sum_shapes = ((rows, 2 * hidden_size), (rows, 128))

    def gate_up(i, arrived, held):
        first, last = i == 0, i == chunks - 1

        def weight_block(b):
            return pl.BlockSpec((hidden_size, width), lambda s, at: (0, at[s * blocks + b] * chunks + i))

        def constant(shape):
            return pl.BlockSpec(shape, lambda s, at: (0, 0))

        return pl.pallas_call(
            functools.partial(expert_kernel, seq_count, blocks, first, last, features),
            grid_spec=pltpu.PrefetchScalarGridSpec(
                num_scalar_prefetch=1,
                grid=(seq_count // blocks,),
                in_specs=[constant((rows, width))] * seq_count
                + [weight_block(b) for b in range(blocks)] * 2
                + [constant(a.shape) for a in held],
                out_specs=constant((rows, hidden_size)) if last else tuple(constant(s) for s in sum_shapes),
                scratch_shapes=[pltpu.VMEM(s, F32) for s in sum_shapes] if last else [],
            ),
            out_shape=jax.ShapeDtypeStruct((rows, hidden_size), BF16)
            if last
            else tuple(jax.ShapeDtypeStruct(s, F32) for s in sum_shapes),
            compiler_params=params(),
            cost_estimate=cost(24 / chunks),
            name="gate_up",
        )(blocks_at, *arrived, *[gate_view] * blocks, *[up_view] * blocks, *held)

    projected, sent, tokens, arrived, sums = [None] * chunks, [None] * chunks, [None] * chunks, [None] * chunks, []
    projected[0] = project(0)
    sent[0] = sum_layers(*projected[0])
    pack_map, mix_high, mix_low = slot_maps(sent[0][0])
    for i in range(chunks):
        if i + 1 < chunks:
            projected[i + 1] = project(i + 1, sent[i][0])
        if i == chunks - 1:
            both = both_cores(after(a, sent[i][0]) for a in arrived[0])
            sums = gate_up(0, both, sums)
            sent[i] = (after(sent[i][0], *sums), sent[i][1])
        tokens[i] = add_layers(*sent[i])
        if i + 1 < chunks:
            sent[i + 1] = sum_layers(*projected[i + 1])
        arrived[i] = dispatch(*tokens[i])
    middle = summed_rows // 2
    own = jnp.concatenate([token[:middle] for token, _ in tokens], axis=1)
    other = swap_cores(own[middle // 2 :])
    own = own[: middle // 2]
    joined = jnp.where(core == 0, jnp.concatenate([own, other], axis=1), jnp.concatenate([other, own], axis=1))
    joined = [joined[d * tok : (d + 1) * tok] for d in range(columns)]
    for i in range(1, chunks):
        both = both_cores([after(a, *sums) for a in arrived[i]])
        if i == chunks - 1:
            joined = [after(a, *arrived[i]) for a in joined]
            both[0] = after(both[0], *joined)
            joined = [joined[0]] + [swap_columns(joined[d], d) for d in range(1, columns)]
        sums = gate_up(i, both, sums)
    expert_hidden = after(sums, *joined)
    tile = 512

    def down(piece, *earlier):
        offset, out_width = piece
        own, *other = pl.pallas_call(
            down_kernel,
            grid=(out_width // tile,),
            out_shape=(jax.ShapeDtypeStruct((rows // 2, out_width), BF16),)
            + (jax.ShapeDtypeStruct((slots, out_width), BF16),) * columns,
            in_specs=[
                whole_block(expert_hidden),
                pl.BlockSpec((hidden_size, tile), lambda n: (0, offset // tile + n)),
            ],
            out_specs=(pl.BlockSpec((rows // 2, tile), lambda n: (0, n)),)
            + (pl.BlockSpec((slots, tile), lambda n: (0, n)),) * columns,
            compiler_params=params(),
            cost_estimate=cost(16 * out_width / features),
            name="down",
        )(after(expert_hidden, *earlier), down_weight[0])
        return own, [swap_cores(a) for a in other]

    def summed(own, other, *earlier):
        own = after(own, *earlier)
        return [
            (own[d * slots : (d + 1) * slots].astype(F32) + other[d].astype(F32)).astype(BF16)
            for d in range(columns)
        ]

    def combine(piece, back):
        out_width = piece[1]
        keep, send = pl.pallas_call(
            functools.partial(combine_kernel, columns),
            grid=(out_width // tile,),
            out_shape=(
                jax.ShapeDtypeStruct((half, out_width), F32),
                jax.ShapeDtypeStruct((half, out_width), BF16),
            ),
            in_specs=[whole_block(mix_high), whole_block(mix_low)]
            + [pl.BlockSpec((slots, tile), lambda n: (0, n))] * columns,
            out_specs=(pl.BlockSpec((half, tile), lambda n: (0, n)),) * 2,
            compiler_params=params(),
            cost_estimate=cost(1),
            name="combine",
        )(mix_high, mix_low, *back)
        return keep, swap_layers(send, distances[0])

    def layer_sum(keep, arrived):
        part = keep + arrived.astype(F32)
        kept = part.shape[0] // 2
        return part[:kept], swap_layers(part[kept:].astype(BF16), distances[-1])

    def finish(piece, part, arrived):
        mine = own_hidden[:, piece[0] : piece[0] + piece[1]].astype(F32)
        return (mine + (part + arrived.astype(F32))).astype(BF16)

    sent, mixed, last = [], [], []
    ahead = down(returns[0])
    for i, piece in enumerate(returns):
        sums = summed(*ahead, *(sent[i - 1] if i else []))
        sent.append([sums[0]] + [swap_columns(sums[d], d) for d in range(1, columns)])
        if i + 1 < len(returns):
            ahead = down(returns[i + 1], *sums)
        if i:
            gate = ahead[1] if i + 1 < len(returns) else sums
            mixed.append(combine(returns[i - 1], [after(a, *gate) for a in sent[i - 1]]))
    earlier = []
    for i in range(len(returns) - 1):
        last.append(layer_sum(mixed[i][0], after(mixed[i][1], *earlier)))
        earlier = [last[i][1]] if i + 2 < len(returns) else [last[i][0]]
    mixed.append(combine(returns[-1], [after(a, *earlier) for a in sent[-1]]))
    last.append(layer_sum(*mixed[-1]))

    joined = jnp.concatenate(joined, axis=0)
    own_hidden = jnp.concatenate(
        [lax.dynamic_slice_in_dim(joined, columns_at[d] * tok, tok, 0) for d in range(columns)], axis=1
    )
    outputs = [finish(piece, *last[i]) for i, piece in enumerate(returns)]
    return jnp.concatenate(outputs, axis=1)


def general(
    queries,
    keys,
    values,
    log_decay,
    residual,
    out_weight,
    gate_weight,
    up_weight,
    down_weight,
    expert_ids,
    route_weights,
):
    seq_count = lax.axis_size("seq")
    span_len = queries.shape[0]
    head_count = log_decay.shape[0]
    head_size = queries.shape[1] // head_count
    query_heads = queries.reshape(span_len, head_count, head_size)
    key_heads = keys.reshape(span_len, head_count, head_size)
    value_heads = values.reshape(span_len, head_count, head_size)
    cumulative = jnp.cumsum(log_decay, axis=1)
    positions = jnp.arange(span_len)
    causal = (positions[:, None] >= positions[None, :])[None]
    spread_log = cumulative[:, :, None] - cumulative[:, None, :]
    weight = jnp.where(causal, jnp.exp(jnp.where(causal, spread_log, 0.0)), 0.0)
    raw_scores = jnp.einsum(
        "thd,shd->hts", query_heads, key_heads, preferred_element_type=jnp.float32
    )
    local_scores = (raw_scores * weight).astype(jnp.bfloat16)
    local_part = jnp.einsum(
        "hts,shd->thd", local_scores, value_heads, preferred_element_type=jnp.float32
    )
    span_total = cumulative[:, -1]
    key_scale = jnp.exp(span_total[:, None] - cumulative)
    weighted_keys = (key_scale.T[:, :, None] * key_heads.astype(jnp.float32)).astype(jnp.bfloat16)
    span_state = jnp.einsum(
        "thd,the->hde", weighted_keys, value_heads, preferred_element_type=jnp.float32
    ).astype(jnp.bfloat16)
    decays = lax.all_gather(span_total[None, :], "seq", axis=0, tiled=True)
    running = jnp.cumsum(decays, axis=0)
    my_index = lax.axis_index("seq")
    before = lax.dynamic_index_in_dim(running, jnp.maximum(my_index - 1, 0), 0, keepdims=False)
    shard_piece = lax.all_gather(span_state[None], "seq", axis=0, tiled=True)
    row_count = shard_piece.shape[0]
    source = jnp.arange(row_count)
    earlier_mask = (source < my_index)[:, None]
    factor = jnp.where(
        earlier_mask, jnp.exp(jnp.where(earlier_mask, before[None, :] - running, 0.0)), 0.0
    )
    prefix = jnp.einsum(
        "nh,nhde->hde", factor, shard_piece.astype(jnp.float32), precision=lax.Precision.HIGHEST
    )
    prefix_low = prefix.astype(jnp.bfloat16)
    weighted_queries = (jnp.exp(cumulative).T[:, :, None] * query_heads.astype(jnp.float32)).astype(
        jnp.bfloat16
    )
    carried_part = jnp.einsum(
        "thd,hde->the", weighted_queries, prefix_low, preferred_element_type=jnp.float32
    )
    mixed_heads = local_part + carried_part
    normed = (
        mixed_heads * lax.rsqrt(jnp.mean(mixed_heads * mixed_heads, axis=-1, keepdims=True) + 1e-06)
    ).astype(jnp.bfloat16)
    normed = normed.reshape(span_len, head_count * head_size)
    partial_out = jnp.dot(
        normed,
        lax.all_gather(out_weight, "seq", axis=1, tiled=True),
        preferred_element_type=jnp.float32,
    )
    attn_out = lax.psum_scatter(
        partial_out.astype(jnp.bfloat16), "mp", scatter_dimension=0, tiled=True
    ).astype(jnp.float32)
    hidden_state = (residual.astype(jnp.float32) + attn_out).astype(jnp.bfloat16)
    hidden_wide = hidden_state.astype(jnp.float32)
    moe_input = (
        hidden_wide * lax.rsqrt(jnp.mean(hidden_wide * hidden_wide, axis=-1, keepdims=True) + 1e-06)
    ).astype(jnp.bfloat16)
    model_width = residual.shape[1]
    experts = seq_count // PAIR
    tok_rows = residual.shape[0]
    capacity = max(2, tok_rows * TOP * 3 // (2 * experts))
    assign_count = tok_rows * TOP
    flat_ids = expert_ids.reshape(-1)
    expert_hot = (flat_ids[:, None] == jnp.arange(experts)[None, :]).astype(jnp.int32)
    slot_rank = jnp.sum((jnp.cumsum(expert_hot, axis=0) - expert_hot) * expert_hot, axis=1)
    target = flat_ids * capacity + slot_rank
    slot_hot = (target[:, None] == jnp.arange(experts * capacity)[None, :]).astype(jnp.float32)
    owner_hot = (
        (jnp.arange(assign_count) // TOP)[:, None] == jnp.arange(tok_rows)[None, :]
    ).astype(jnp.float32)
    dispatch_map = jnp.einsum("as,at->st", slot_hot, owner_hot).astype(jnp.bfloat16)
    packed = jnp.dot(dispatch_map, moe_input, preferred_element_type=jnp.float32).astype(
        jnp.bfloat16
    )
    outgoing = jnp.broadcast_to(
        packed.reshape(experts, 1, capacity, model_width), (experts, PAIR, capacity, model_width)
    )
    outgoing = outgoing.reshape(seq_count, capacity, model_width)
    incoming = lax.all_to_all(outgoing, "seq", split_axis=0, concat_axis=0, tiled=True)
    expert_rows = incoming.reshape(seq_count * capacity, model_width)
    gate_matrix = gate_weight[0]
    up_matrix = up_weight[0]
    down_matrix = down_weight[0]
    shard_piece = lax.all_gather(expert_rows, "mp", axis=0, tiled=True)
    gate_value = jnp.dot(shard_piece, gate_matrix, preferred_element_type=jnp.float32)
    lifted = jnp.dot(shard_piece, up_matrix, preferred_element_type=jnp.float32)
    hidden_rows = (jax.nn.silu(gate_value) * lifted).astype(jnp.bfloat16)
    half_out = lax.psum_scatter(
        jnp.dot(hidden_rows, down_matrix, preferred_element_type=jnp.float32).astype(jnp.bfloat16),
        "mp",
        scatter_dimension=0,
        tiled=True,
    )
    returned = lax.all_to_all(
        half_out.reshape(seq_count, capacity, model_width),
        "seq",
        split_axis=0,
        concat_axis=0,
        tiled=True,
    )
    expert_out = jnp.sum(
        returned.reshape(experts, PAIR, capacity, model_width).astype(jnp.float32), axis=1
    )
    expert_out = expert_out.reshape(experts * capacity, model_width)
    weighted = route_weights.reshape(-1)[:, None] * slot_hot
    combine_map = jnp.einsum("at,as->ts", owner_hot, weighted, precision=lax.Precision.HIGHEST)
    expert_mix = jnp.dot(combine_map, expert_out, precision=lax.Precision.HIGHEST)
    return (hidden_wide + expert_mix).astype(jnp.bfloat16)


def cuts(tile, parts):
    return [(sum(parts[:i]) * tile, part * tile) for i, part in enumerate(parts)]


def fits(mesh, tok, features, block, chunks):
    layers, seq_count = mesh.shape["mp"], mesh.shape["seq"]
    powers = seq_count & (seq_count - 1) == 0 and seq_count > PAIR
    return powers and layers == 4 and tok % 16 == 0 and block % (128 * chunks) == 0 and features % (512 * 12) == 0


def solution(mesh):
    placed = (
        P("seq", "mp"),
        P("seq", "mp"),
        P("seq", "mp"),
        P("mp", "seq"),
        P(("seq", "mp"), None),
        P("mp", "seq"),
        P("seq", None, "mp"),
        P("seq", None, "mp"),
        P("seq", "mp", None),
        P(("seq", "mp"), None),
        P(("seq", "mp"), None),
    )
    chunks = 3

    def per_device(*args):
        residual, out_weight = args[4], args[5]
        features, block = residual.shape[1], out_weight.shape[1]
        if fits(mesh, residual.shape[0], features, block, chunks):
            return tiled(*args, chunks=chunks, returns=cuts(features // 12, [2, 4, 4, 2]))
        return general(*args)

    return jax.shard_map(
        per_device, mesh=mesh, in_specs=placed, out_specs=P(("seq", "mp"), None), check_vma=False
    )
```

```python
import functools

import jax
import jax.numpy as jnp
from jax import lax
from jax.experimental import pallas as pl
from jax.experimental.pallas import tpu as pltpu
from jax.sharding import PartitionSpec as P

TOP = 2
PAIR = 2
VMEM_LIMIT = 44 * 1024 * 1024
EXTRA_ROWS = 16
ROUTE_ROWS = 10
HIGH = lax.Precision.HIGHEST
F32 = jnp.float32
BF16 = jnp.bfloat16


def params():
    return pltpu.CompilerParams(vmem_limit_bytes=VMEM_LIMIT)


def cost(microseconds):
    return pl.CostEstimate(flops=0, bytes_accessed=int(microseconds * 3.69e6), transcendentals=0)


def after(array, *earlier):
    return lax.optimization_barrier((array,) + earlier)[0]


def swap_columns(array, distance):
    count = lax.axis_size("seq")
    return lax.ppermute(array, "seq", [(i, i ^ (PAIR * distance)) for i in range(count)])


def swap_cores(array):
    count = lax.axis_size("seq")
    return lax.ppermute(array, "seq", [(i, i ^ 1) for i in range(count)])


def swap_layers(array, distance):
    count = lax.axis_size("mp")
    return lax.ppermute(array, "mp", [(i, i ^ distance) for i in range(count)])


def local_kernel(column_ref, q_ref, k_ref, v_ref, decay_ref, residual_ref, local_ref, weighted_ref, *message_refs):
    span = q_ref.shape[0]
    heads = decay_ref.shape[0]
    size = q_ref.shape[1] // heads
    row = lax.broadcasted_iota(jnp.int32, (span, span), 0)
    col = lax.broadcasted_iota(jnp.int32, (span, span), 1)
    causal = row >= col
    decay = decay_ref[...]
    along = jnp.dot(decay, (row <= col).astype(F32), precision=HIGH, preferred_element_type=F32)
    down = lax.dot_general(
        causal.astype(F32), decay, (((1,), (1,)), ((), ())), precision=HIGH, preferred_element_type=F32
    )
    extra = lax.broadcasted_iota(jnp.int32, (EXTRA_ROWS, size), 0)
    for h in range(heads):
        cols = slice(h * size, (h + 1) * size)
        q, k, v = q_ref[:, cols], k_ref[:, cols], v_ref[:, cols]
        here = down[:, h : h + 1]
        spread = here - along[h : h + 1, :]
        weight = jnp.where(causal, jnp.exp(jnp.where(causal, spread, 0.0)), 0.0)
        raw = lax.dot_general(q, k, (((1,), (1,)), ((), ())), preferred_element_type=F32)
        local_ref[:, cols] = jnp.dot((raw * weight).astype(BF16), v, preferred_element_type=F32)
        total = along[h : h + 1, span - 1 : span]
        scaled = (jnp.exp(total - here) * k.astype(F32)).astype(BF16)
        state = lax.dot_general(scaled, v, (((0,), (0,)), ((), ())), preferred_element_type=F32).astype(BF16)
        first = total.astype(BF16).astype(F32)
        second = (total - first).astype(BF16).astype(F32)
        third = total - first - second
        pieces = jnp.where(extra == 0, first, jnp.where(extra == 1, second, jnp.where(extra == 2, third, 0.0)))
        at = h * (size + EXTRA_ROWS)
        for message in message_refs:
            message[at : at + size, :] = state
            message[at + size : at + size + EXTRA_ROWS, :] = pieces.astype(BF16)
        weighted_ref[:, cols] = (jnp.exp(here) * q.astype(F32)).astype(BF16)
    tok = residual_ref.shape[0]
    first = heads * (size + EXTRA_ROWS)
    for d, message in enumerate(message_refs):
        parts = (message.shape[0] - first) // tok
        for b in range(parts):
            at = pl.multiple_of((column_ref[d] * parts + b) * size, size)
            message[first + b * tok : first + (b + 1) * tok, :] = residual_ref[:, pl.ds(at, size)]


def prefix_kernel(count, heads, layers, *refs):
    row_ref, between_ref, earlier_ref, local_ref, weighted_ref, route_ref = refs[:6]
    message_refs = refs[6 : 6 + count]
    out_ref, totals, held = refs[6 + count :]
    span = local_ref.shape[0]
    size = local_ref.shape[1] // heads
    tall = size + EXTRA_ROWS
    for p in range(count):
        for h in range(heads):
            extra = message_refs[p][h * tall + size : (h + 1) * tall, :].astype(F32)
            totals[p : p + 1, h * size : (h + 1) * size] = jnp.sum(extra, axis=0, keepdims=True)
    gap = jnp.dot(between_ref[...], totals[...], precision=HIGH, preferred_element_type=F32)
    totals[...] = jnp.exp(gap) * earlier_ref[...]
    for h in range(heads):
        cols = slice(h * size, (h + 1) * size)
        prefix = jnp.zeros((size, size), F32)
        for p in range(count):
            prefix += totals[p : p + 1, cols] * message_refs[p][h * tall : h * tall + size, :].astype(F32)
        mixed = local_ref[:, cols] + jnp.dot(
            weighted_ref[:, cols], prefix.astype(BF16), preferred_element_type=F32
        )
        mean = jnp.mean(mixed * mixed, axis=-1, keepdims=True)
        held[:, cols] = (mixed * lax.rsqrt(mean + 1e-06)).astype(BF16)
    rows = span // layers
    for r in range(layers):
        start = pl.multiple_of(row_ref[r] * rows, rows)
        out_ref[r * rows : (r + 1) * rows, :] = held[pl.ds(start, rows), :]
    out_ref[span:, :] = jnp.zeros((EXTRA_ROWS, heads * size), BF16)
    out_ref[span:, :span] = route_ref[...]


def map_kernel(count, columns, capacity, tok, column_ref, *refs):
    row_refs, (pack_ref, high_ref, low_ref) = refs[:count], refs[count:]
    slots, span = high_ref.shape[0] // columns, high_ref.shape[1]
    row = lax.broadcasted_iota(jnp.int32, (slots, span), 0)
    lane = lax.broadcasted_iota(jnp.int32, (1, span), 1)
    base = (lane // tok) * capacity
    for p in range(count):
        route = row_refs[p][span : span + EXTRA_ROWS, :span].astype(F32)
        for d in range(columns):
            expert = column_ref[d]
            hit, gain = None, None
            for k in range(TOP):
                named = route[k : k + 1].astype(jnp.int32) == expert
                rank = route[TOP + k : TOP + k + 1].astype(jnp.int32)
                at = 2 * TOP + 3 * k
                value = route[at : at + 1] + route[at + 1 : at + 2] + route[at + 2 : at + 3]
                here = jnp.where(named, base + rank, -1) == row
                weight = jnp.where(here, value, 0.0)
                hit = here if hit is None else hit | here
                gain = weight if gain is None else gain + weight
            pack_ref[p, d * slots : (d + 1) * slots, :] = jnp.where(hit, 1.0, 0.0).astype(BF16)
            if p == 0:
                high = gain.astype(BF16)
                high_ref[d * slots : (d + 1) * slots, :] = high
                low_ref[d * slots : (d + 1) * slots, :] = (gain - high.astype(F32)).astype(BF16)


def project_kernel(count, layers, tok, chunk, core_ref, *refs):
    row_refs, message_refs = refs[:count], refs[count : 2 * count]
    weight_ref, keep_ref, send_ref = refs[2 * count :]
    span = layers * tok
    rows = jnp.concatenate([ref[:span] for ref in row_refs], axis=0)
    part = jnp.dot(rows, weight_ref[...], preferred_element_type=F32).astype(BF16)
    lanes = message_refs[0].shape[1]
    pieces = weight_ref.shape[1] // lanes
    for r in range(layers):
        for p in range(count):
            to = (r % (layers // 2)) * count * tok + p * tok
            here = part[p * span + r * tok : p * span + (r + 1) * tok]
            if r >= layers // 2:
                send_ref[to : to + tok, :] = here
            elif r > 0:
                keep_ref[to : to + tok, :] = here.astype(F32)
            else:
                for b in range(pieces):
                    at = pl.multiple_of(core_ref[0] + (chunk * pieces + b) * tok, tok)
                    own = message_refs[p][pl.ds(at, tok), :].astype(F32)
                    cols = slice(b * lanes, (b + 1) * lanes)
                    keep_ref[to : to + tok, cols] = here[:, cols].astype(F32) + own


def pack_kernel(count, layers, place_ref, map_ref, near_ref, far_ref, *out_refs):
    slots = out_refs[0].shape[0] // count
    tok = near_ref.shape[0] // (layers // 2) // count
    for p in range(count):
        pieces = [
            ref[r * count * tok + p * tok : r * count * tok + (p + 1) * tok, :]
            for ref in (near_ref, far_ref)
            for r in range(layers // 2)
        ]
        tokens = jnp.concatenate(pieces, axis=0)
        packed = jnp.dot(map_ref[p], tokens, preferred_element_type=F32).astype(BF16)
        start = pl.multiple_of(place_ref[p] * slots, slots)
        for d in range(len(out_refs)):
            out_refs[d][pl.ds(start, slots), :] = packed[d * slots : (d + 1) * slots]


def expert_kernel(pieces, blocks, first, last, features, place_ref, *refs):
    x_refs = refs[:pieces]
    gate_refs, up_refs = refs[pieces : pieces + blocks], refs[pieces + blocks : pieces + 2 * blocks]
    rest = refs[pieces + 2 * blocks :]
    if not first:
        sum_in, square_in = rest[:2]
        rest = rest[2:]
    if last:
        out_ref, sum_ref, square_ref = rest
    else:
        sum_ref, square_ref = rest
    size = gate_refs[0].shape[0]
    even = size // 128 * 128
    lanes = square_ref.shape[1]
    step = pl.program_id(0)

    for s in range(pieces // blocks):

        @pl.when(step == s)
        def _(s=s):
            x = jnp.concatenate([ref[...] for ref in x_refs[s * blocks : (s + 1) * blocks]], axis=1)
            gate = jnp.concatenate([ref[...] for ref in gate_refs], axis=1)
            up = jnp.concatenate([ref[...] for ref in up_refs], axis=1)
            both = jnp.concatenate([gate[:even], up[:even], gate[even:], up[even:]], axis=0)
            sums = lax.dot_general(x, both, (((1,), (1,)), ((), ())), preferred_element_type=F32)
            wide = x.astype(F32)
            squares = wide[:, :lanes] * wide[:, :lanes]
            for i in range(1, x.shape[1] // lanes):
                part = wide[:, i * lanes : (i + 1) * lanes]
                squares += part * part
            if s > 0:
                sum_ref[...] += sums
                square_ref[...] += squares
            else:
                sum_ref[...] = sums if first else sum_in[...] + sums
                square_ref[...] = squares if first else square_in[...] + squares

    if last:

        @pl.when(step == pl.num_programs(0) - 1)
        def _():
            slots = out_ref.shape[0] // pieces

            def activate(gate, up, scale):
                gate = gate * scale
                return (gate / (1.0 + jnp.exp(-gate)) * (up * scale)).astype(BF16)

            for p in range(pieces):
                rows = pl.ds(pl.multiple_of(place_ref[p] * slots, slots), slots)
                to = slice(p * slots, (p + 1) * slots)
                mean = jnp.sum(square_ref[rows, :], axis=1, keepdims=True) / features
                scale = lax.rsqrt(mean + 1e-06)
                out_ref[to, :even] = activate(sum_ref[rows, :even], sum_ref[rows, even : 2 * even], scale)
                if even < size:
                    tail = sum_ref[rows, 2 * even :]
                    out_ref[to, even:] = activate(tail[:, : size - even], tail[:, size - even :], scale)


def down_kernel(hidden_ref, weight_ref, own_ref, *other_refs):
    half = own_ref.shape[0]
    out = jnp.dot(hidden_ref[...], weight_ref[...], preferred_element_type=F32).astype(BF16)
    own_ref[...] = out[:half]
    rows = half // len(other_refs)
    for d, ref in enumerate(other_refs):
        ref[...] = out[half + d * rows : half + (d + 1) * rows]


def combine_kernel(count, high_ref, low_ref, *refs):
    x_refs = refs[:count]
    keep_ref, send_ref = refs[count:]
    half = keep_ref.shape[0]
    x = jnp.concatenate([ref[...] for ref in x_refs], axis=0)
    out = lax.dot_general(high_ref[...], x, (((0,), (0,)), ((), ())), preferred_element_type=F32)
    out += lax.dot_general(low_ref[...], x, (((0,), (0,)), ((), ())), preferred_element_type=F32)
    keep_ref[...] = out[:half]
    send_ref[...] = out[half:].astype(BF16)


def whole_block(array):
    return pl.BlockSpec(array.shape, lambda *_: (0,) * array.ndim)


def tiled(
    queries, keys, values, log_decay, residual, out_weight, gate_weight, up_weight, down_weight, expert_ids,
    route_weights, chunks, returns,
):
    seq_count, layers = lax.axis_size("seq"), lax.axis_size("mp")
    me, layer = lax.axis_index("seq"), lax.axis_index("mp")
    columns = seq_count // PAIR
    column = me // PAIR
    span, heads = queries.shape[0], log_decay.shape[0]
    size = queries.shape[1] // heads
    features = residual.shape[1]
    hidden_size = gate_weight.shape[2]
    tok = residual.shape[0]
    half = span // 2
    block = out_weight.shape[1]
    width = block // chunks
    capacity = max(2, tok * TOP * 3 // (2 * columns))
    slots = layers * capacity
    distances = [1 << i for i in range((layers - 1).bit_length())]
    order = [0]
    for d in reversed(distances):
        order = order + [b ^ d for b in order]

    away = [PAIR * (p % columns) + p // columns for p in range(seq_count)]
    blocks_at = jnp.stack([me ^ a for a in away]).astype(jnp.int32)
    rows_at = jnp.stack([layer ^ r for r in order]).astype(jnp.int32)
    columns_at = jnp.stack([column ^ d for d in range(columns)]).astype(jnp.int32)

    def across(array):
        return [array] + [swap_columns(array, d) for d in range(1, columns)]

    def both_cores(arrays):
        arrays = list(arrays)
        return arrays + [swap_cores(a) for a in arrays]

    smem = pl.BlockSpec(memory_space=pltpu.SMEM)
    vmem = pl.BlockSpec(memory_space=pltpu.VMEM)
    residual_at = heads * (size + EXTRA_ROWS)
    message = (residual_at + PAIR * block // size * tok, size)
    local_part, weighted_queries, *messages = pl.pallas_call(
        local_kernel,
        out_shape=(
            jax.ShapeDtypeStruct((span, heads * size), F32),
            jax.ShapeDtypeStruct((span, heads * size), BF16),
        )
        + (jax.ShapeDtypeStruct(message, BF16),) * columns,
        grid=(1,),
        in_specs=[smem] + [whole_block(a) for a in (queries, keys, values, log_decay, residual)],
        out_specs=(pl.BlockSpec((span, heads * size), lambda n: (0, 0)),) * 2
        + (pl.BlockSpec(message, lambda n: (0, 0)),) * columns,
        compiler_params=params(),
        cost_estimate=cost(1.5),
        name="local_attention",
    )(columns_at, queries, keys, values, log_decay, residual)
    messages = [messages[0]] + [swap_columns(messages[d], d) for d in range(1, columns)]

    flat = after(expert_ids, local_part).reshape(-1)
    count = flat.shape[0]
    before = jnp.arange(count)[:, None] > jnp.arange(count)[None, :]
    rank = jnp.sum((before & (flat[:, None] == flat[None, :])).astype(jnp.int32), axis=1).reshape(tok, TOP)
    first = lax.reduce_precision(route_weights, 8, 7)
    second = lax.reduce_precision(route_weights - first, 8, 7)
    third = route_weights - first - second
    parts = jnp.stack([first, second, third], axis=2).reshape(tok, 3 * TOP)
    route = jnp.concatenate([expert_ids.astype(F32), rank.astype(F32), parts], axis=1).T.astype(BF16)
    route = jnp.pad(route, ((0, EXTRA_ROWS - ROUTE_ROWS), (0, 0)))
    for d in reversed(distances):
        route = jnp.concatenate([route, swap_layers(route, d)], axis=1)

    messages = both_cores([after(a, route) for a in messages])
    between = ((blocks_at[:, None] < blocks_at[None, :]) & (blocks_at[None, :] < me)).astype(F32)
    earlier = jnp.broadcast_to((blocks_at < me).astype(F32)[:, None], (seq_count, heads * size))
    normed = pl.pallas_call(
        functools.partial(prefix_kernel, seq_count, heads, layers),
        out_shape=jax.ShapeDtypeStruct((span + EXTRA_ROWS, heads * size), BF16),
        in_specs=[smem] + [vmem] * (5 + seq_count),
        out_specs=vmem,
        scratch_shapes=[pltpu.VMEM((seq_count, heads * size), F32), pltpu.VMEM((span, heads * size), BF16)],
        compiler_params=params(),
        cost_estimate=cost(1.2),
        name="prefix_attention",
    )(rows_at, between, earlier, local_part, weighted_queries, route, *messages)
    normed = both_cores(across(normed))

    core = me % PAIR
    core_at = (residual_at + core * (block // size * tok)).reshape(1).astype(jnp.int32)

    def slot_maps(*earlier):
        return pl.pallas_call(
            functools.partial(map_kernel, seq_count, columns, capacity, tok),
            out_shape=(
                jax.ShapeDtypeStruct((seq_count, columns * slots, span), BF16),
                jax.ShapeDtypeStruct((columns * slots, span), BF16),
                jax.ShapeDtypeStruct((columns * slots, span), BF16),
            ),
            in_specs=[smem] + [vmem] * seq_count,
            out_specs=(vmem,) * 3,
            compiler_params=params(),
            cost_estimate=cost(1.3),
            name="slot_maps",
        )(columns_at, after(normed[0], *earlier), *normed[1:])

    rows = seq_count * slots
    summed_rows = seq_count * half
    gate_view, up_view = gate_weight[0].T, up_weight[0].T

    def project(i, *earlier):
        keep, send = pl.pallas_call(
            functools.partial(project_kernel, seq_count, layers, tok, i),
            grid=(1,),
            out_shape=(
                jax.ShapeDtypeStruct((summed_rows, width), F32),
                jax.ShapeDtypeStruct((summed_rows, width), BF16),
            ),
            in_specs=[smem] + [whole_block(a) for a in (*normed, *messages)]
            + [pl.BlockSpec((heads * size, width), lambda n: (0, i))],
            out_specs=(pl.BlockSpec((summed_rows, width), lambda n: (0, 0)),) * 2,
            compiler_params=params(),
            cost_estimate=cost(1),
            name="project",
        )(core_at, after(normed[0], *earlier), *normed[1:], *messages, out_weight)
        return keep, swap_layers(send, distances[0])

    def sum_layers(keep, arrived):
        part = (keep + arrived.astype(F32)).astype(BF16)
        return part, swap_layers(part, distances[-1])

    def add_layers(part, other):
        middle = other.shape[0] // 2
        other = jnp.concatenate([other[middle:], other[:middle]], axis=0)
        token = (part.astype(F32) + other.astype(F32)).astype(BF16)
        return token, swap_layers(token, distances[0])

    def dispatch(token, far):
        packed = pl.pallas_call(
            functools.partial(pack_kernel, seq_count, layers),
            out_shape=(jax.ShapeDtypeStruct((rows, width), BF16),) * columns,
            in_specs=[smem] + [vmem] * 3,
            out_specs=(vmem,) * columns,
            compiler_params=params(),
            cost_estimate=cost(1),
            name="pack",
        )(blocks_at, pack_map, token, far)
        return [packed[0]] + [swap_columns(packed[d], d) for d in range(1, columns)]

    blocks = columns
    sum_shapes = ((rows, 2 * hidden_size), (rows, 128))

    def gate_up(i, arrived, held):
        first, last = i == 0, i == chunks - 1

        def weight_block(b):
            return pl.BlockSpec((hidden_size, width), lambda s, at: (0, at[s * blocks + b] * chunks + i))

        def constant(shape):
            return pl.BlockSpec(shape, lambda s, at: (0, 0))

        return pl.pallas_call(
            functools.partial(expert_kernel, seq_count, blocks, first, last, features),
            grid_spec=pltpu.PrefetchScalarGridSpec(
                num_scalar_prefetch=1,
                grid=(seq_count // blocks,),
                in_specs=[constant((rows, width))] * seq_count
                + [weight_block(b) for b in range(blocks)] * 2
                + [constant(a.shape) for a in held],
                out_specs=constant((rows, hidden_size)) if last else tuple(constant(s) for s in sum_shapes),
                scratch_shapes=[pltpu.VMEM(s, F32) for s in sum_shapes] if last else [],
            ),
            out_shape=jax.ShapeDtypeStruct((rows, hidden_size), BF16)
            if last
            else tuple(jax.ShapeDtypeStruct(s, F32) for s in sum_shapes),
            compiler_params=params(),
            cost_estimate=cost(24 / chunks),
            name="gate_up",
        )(blocks_at, *arrived, *[gate_view] * blocks, *[up_view] * blocks, *held)

    projected, sent, tokens, arrived, sums = [None] * chunks, [None] * chunks, [None] * chunks, [None] * chunks, []
    projected[0] = project(0)
    sent[0] = sum_layers(*projected[0])
    pack_map, mix_high, mix_low = slot_maps(sent[0][0])
    for i in range(chunks):
        if i + 1 < chunks:
            projected[i + 1] = project(i + 1, sent[i][0])
        if i == chunks - 1:
            both = both_cores(after(a, sent[i][0]) for a in arrived[0])
            sums = gate_up(0, both, sums)
            sent[i] = (after(sent[i][0], *sums), sent[i][1])
        tokens[i] = add_layers(*sent[i])
        if i + 1 < chunks:
            sent[i + 1] = sum_layers(*projected[i + 1])
        arrived[i] = dispatch(*tokens[i])
    middle = summed_rows // 2
    own = jnp.concatenate([token[:middle] for token, _ in tokens], axis=1)
    other = swap_cores(own[middle // 2 :])
    own = own[: middle // 2]
    joined = jnp.where(core == 0, jnp.concatenate([own, other], axis=1), jnp.concatenate([other, own], axis=1))
    joined = [joined[d * tok : (d + 1) * tok] for d in range(columns)]
    for i in range(1, chunks):
        both = both_cores([after(a, *sums) for a in arrived[i]])
        if i == chunks - 1:
            joined = [after(a, *arrived[i]) for a in joined]
            both[0] = after(both[0], *joined)
            joined = [joined[0]] + [swap_columns(joined[d], d) for d in range(1, columns)]
        sums = gate_up(i, both, sums)
    expert_hidden = after(sums, *joined)
    tile = 1024

    def down(piece, *earlier):
        offset, out_width = piece
        own, *other = pl.pallas_call(
            down_kernel,
            grid=(out_width // tile,),
            out_shape=(jax.ShapeDtypeStruct((rows // 2, out_width), BF16),)
            + (jax.ShapeDtypeStruct((slots, out_width), BF16),) * columns,
            in_specs=[
                whole_block(expert_hidden),
                pl.BlockSpec((hidden_size, tile), lambda n: (0, offset // tile + n)),
            ],
            out_specs=(pl.BlockSpec((rows // 2, tile), lambda n: (0, n)),)
            + (pl.BlockSpec((slots, tile), lambda n: (0, n)),) * columns,
            compiler_params=params(),
            cost_estimate=cost(16 * out_width / features),
            name="down",
        )(after(expert_hidden, *earlier), down_weight[0])
        return own, [swap_cores(a) for a in other]

    def summed(own, other, *earlier):
        own = after(own, *earlier)
        return [
            (own[d * slots : (d + 1) * slots].astype(F32) + other[d].astype(F32)).astype(BF16)
            for d in range(columns)
        ]

    def combine(piece, back):
        out_width = piece[1]
        keep, send = pl.pallas_call(
            functools.partial(combine_kernel, columns),
            grid=(out_width // tile,),
            out_shape=(
                jax.ShapeDtypeStruct((half, out_width), F32),
                jax.ShapeDtypeStruct((half, out_width), BF16),
            ),
            in_specs=[whole_block(mix_high), whole_block(mix_low)]
            + [pl.BlockSpec((slots, tile), lambda n: (0, n))] * columns,
            out_specs=(pl.BlockSpec((half, tile), lambda n: (0, n)),) * 2,
            compiler_params=params(),
            cost_estimate=cost(1),
            name="combine",
        )(mix_high, mix_low, *back)
        return keep, swap_layers(send, distances[0])

    def layer_sum(keep, arrived):
        part = keep + arrived.astype(F32)
        kept = part.shape[0] // 2
        return part[:kept], swap_layers(part[kept:].astype(BF16), distances[-1])

    def finish(piece, part, arrived):
        mine = own_hidden[:, piece[0] : piece[0] + piece[1]].astype(F32)
        return (mine + (part + arrived.astype(F32))).astype(BF16)

    sent, mixed, last = [], [], []
    ahead = down(returns[0])
    for i, piece in enumerate(returns):
        sums = summed(*ahead, *(sent[i - 1] if i else []))
        sent.append([sums[0]] + [swap_columns(sums[d], d) for d in range(1, columns)])
        if i + 1 < len(returns):
            ahead = down(returns[i + 1], *sums)
        if i:
            gate = ahead[1] if i + 1 < len(returns) else sums
            mixed.append(combine(returns[i - 1], [after(a, *gate) for a in sent[i - 1]]))
    earlier = []
    for i in range(len(returns) - 1):
        last.append(layer_sum(mixed[i][0], after(mixed[i][1], *earlier)))
        earlier = [last[i][1]] if i + 2 < len(returns) else [last[i][0]]
    mixed.append(combine(returns[-1], [after(a, *earlier) for a in sent[-1]]))
    last.append(layer_sum(*mixed[-1]))

    joined = jnp.concatenate(joined, axis=0)
    own_hidden = jnp.concatenate(
        [lax.dynamic_slice_in_dim(joined, columns_at[d] * tok, tok, 0) for d in range(columns)], axis=1
    )
    outputs = [finish(piece, *last[i]) for i, piece in enumerate(returns)]
    return jnp.concatenate(outputs, axis=1)


def general(
    queries,
    keys,
    values,
    log_decay,
    residual,
    out_weight,
    gate_weight,
    up_weight,
    down_weight,
    expert_ids,
    route_weights,
):
    seq_count = lax.axis_size("seq")
    span_len = queries.shape[0]
    head_count = log_decay.shape[0]
    head_size = queries.shape[1] // head_count
    query_heads = queries.reshape(span_len, head_count, head_size)
    key_heads = keys.reshape(span_len, head_count, head_size)
    value_heads = values.reshape(span_len, head_count, head_size)
    cumulative = jnp.cumsum(log_decay, axis=1)
    positions = jnp.arange(span_len)
    causal = (positions[:, None] >= positions[None, :])[None]
    spread_log = cumulative[:, :, None] - cumulative[:, None, :]
    weight = jnp.where(causal, jnp.exp(jnp.where(causal, spread_log, 0.0)), 0.0)
    raw_scores = jnp.einsum(
        "thd,shd->hts", query_heads, key_heads, preferred_element_type=jnp.float32
    )
    local_scores = (raw_scores * weight).astype(jnp.bfloat16)
    local_part = jnp.einsum(
        "hts,shd->thd", local_scores, value_heads, preferred_element_type=jnp.float32
    )
    span_total = cumulative[:, -1]
    key_scale = jnp.exp(span_total[:, None] - cumulative)
    weighted_keys = (key_scale.T[:, :, None] * key_heads.astype(jnp.float32)).astype(jnp.bfloat16)
    span_state = jnp.einsum(
        "thd,the->hde", weighted_keys, value_heads, preferred_element_type=jnp.float32
    ).astype(jnp.bfloat16)
    decays = lax.all_gather(span_total[None, :], "seq", axis=0, tiled=True)
    running = jnp.cumsum(decays, axis=0)
    my_index = lax.axis_index("seq")
    before = lax.dynamic_index_in_dim(running, jnp.maximum(my_index - 1, 0), 0, keepdims=False)
    shard_piece = lax.all_gather(span_state[None], "seq", axis=0, tiled=True)
    row_count = shard_piece.shape[0]
    source = jnp.arange(row_count)
    earlier_mask = (source < my_index)[:, None]
    factor = jnp.where(
        earlier_mask, jnp.exp(jnp.where(earlier_mask, before[None, :] - running, 0.0)), 0.0
    )
    prefix = jnp.einsum(
        "nh,nhde->hde", factor, shard_piece.astype(jnp.float32), precision=lax.Precision.HIGHEST
    )
    prefix_low = prefix.astype(jnp.bfloat16)
    weighted_queries = (jnp.exp(cumulative).T[:, :, None] * query_heads.astype(jnp.float32)).astype(
        jnp.bfloat16
    )
    carried_part = jnp.einsum(
        "thd,hde->the", weighted_queries, prefix_low, preferred_element_type=jnp.float32
    )
    mixed_heads = local_part + carried_part
    normed = (
        mixed_heads * lax.rsqrt(jnp.mean(mixed_heads * mixed_heads, axis=-1, keepdims=True) + 1e-06)
    ).astype(jnp.bfloat16)
    normed = normed.reshape(span_len, head_count * head_size)
    partial_out = jnp.dot(
        normed,
        lax.all_gather(out_weight, "seq", axis=1, tiled=True),
        preferred_element_type=jnp.float32,
    )
    attn_out = lax.psum_scatter(
        partial_out.astype(jnp.bfloat16), "mp", scatter_dimension=0, tiled=True
    ).astype(jnp.float32)
    hidden_state = (residual.astype(jnp.float32) + attn_out).astype(jnp.bfloat16)
    hidden_wide = hidden_state.astype(jnp.float32)
    moe_input = (
        hidden_wide * lax.rsqrt(jnp.mean(hidden_wide * hidden_wide, axis=-1, keepdims=True) + 1e-06)
    ).astype(jnp.bfloat16)
    model_width = residual.shape[1]
    experts = seq_count // PAIR
    tok_rows = residual.shape[0]
    capacity = max(2, tok_rows * TOP * 3 // (2 * experts))
    assign_count = tok_rows * TOP
    flat_ids = expert_ids.reshape(-1)
    expert_hot = (flat_ids[:, None] == jnp.arange(experts)[None, :]).astype(jnp.int32)
    slot_rank = jnp.sum((jnp.cumsum(expert_hot, axis=0) - expert_hot) * expert_hot, axis=1)
    target = flat_ids * capacity + slot_rank
    slot_hot = (target[:, None] == jnp.arange(experts * capacity)[None, :]).astype(jnp.float32)
    owner_hot = (
        (jnp.arange(assign_count) // TOP)[:, None] == jnp.arange(tok_rows)[None, :]
    ).astype(jnp.float32)
    dispatch_map = jnp.einsum("as,at->st", slot_hot, owner_hot).astype(jnp.bfloat16)
    packed = jnp.dot(dispatch_map, moe_input, preferred_element_type=jnp.float32).astype(
        jnp.bfloat16
    )
    outgoing = jnp.broadcast_to(
        packed.reshape(experts, 1, capacity, model_width), (experts, PAIR, capacity, model_width)
    )
    outgoing = outgoing.reshape(seq_count, capacity, model_width)
    incoming = lax.all_to_all(outgoing, "seq", split_axis=0, concat_axis=0, tiled=True)
    expert_rows = incoming.reshape(seq_count * capacity, model_width)
    gate_matrix = gate_weight[0]
    up_matrix = up_weight[0]
    down_matrix = down_weight[0]
    shard_piece = lax.all_gather(expert_rows, "mp", axis=0, tiled=True)
    gate_value = jnp.dot(shard_piece, gate_matrix, preferred_element_type=jnp.float32)
    lifted = jnp.dot(shard_piece, up_matrix, preferred_element_type=jnp.float32)
    hidden_rows = (jax.nn.silu(gate_value) * lifted).astype(jnp.bfloat16)
    half_out = lax.psum_scatter(
        jnp.dot(hidden_rows, down_matrix, preferred_element_type=jnp.float32).astype(jnp.bfloat16),
        "mp",
        scatter_dimension=0,
        tiled=True,
    )
    returned = lax.all_to_all(
        half_out.reshape(seq_count, capacity, model_width),
        "seq",
        split_axis=0,
        concat_axis=0,
        tiled=True,
    )
    expert_out = jnp.sum(
        returned.reshape(experts, PAIR, capacity, model_width).astype(jnp.float32), axis=1
    )
    expert_out = expert_out.reshape(experts * capacity, model_width)
    weighted = route_weights.reshape(-1)[:, None] * slot_hot
    combine_map = jnp.einsum("at,as->ts", owner_hot, weighted, precision=lax.Precision.HIGHEST)
    expert_mix = jnp.dot(combine_map, expert_out, precision=lax.Precision.HIGHEST)
    return (hidden_wide + expert_mix).astype(jnp.bfloat16)


def cuts(tile, parts):
    return [(sum(parts[:i]) * tile, part * tile) for i, part in enumerate(parts)]


def fits(mesh, tok, features, block, chunks):
    layers, seq_count = mesh.shape["mp"], mesh.shape["seq"]
    powers = seq_count & (seq_count - 1) == 0 and seq_count > PAIR
    return powers and layers == 4 and tok % 16 == 0 and block % (128 * chunks) == 0 and features % (512 * 12) == 0


def solution(mesh):
    placed = (
        P("seq", "mp"),
        P("seq", "mp"),
        P("seq", "mp"),
        P("mp", "seq"),
        P(("seq", "mp"), None),
        P("mp", "seq"),
        P("seq", None, "mp"),
        P("seq", None, "mp"),
        P("seq", "mp", None),
        P(("seq", "mp"), None),
        P(("seq", "mp"), None),
    )
    chunks = 3

    def per_device(*args):
        residual, out_weight = args[4], args[5]
        features, block = residual.shape[1], out_weight.shape[1]
        if fits(mesh, residual.shape[0], features, block, chunks):
            return tiled(*args, chunks=chunks, returns=cuts(features // 12, [2, 4, 4, 2]))
        return general(*args)

    return jax.shard_map(
        per_device, mesh=mesh, in_specs=placed, out_specs=P(("seq", "mp"), None), check_vma=False
    )
```

```python
import functools

import jax
import jax.numpy as jnp
from jax import lax
from jax.experimental import pallas as pl
from jax.experimental.pallas import tpu as pltpu
from jax.sharding import PartitionSpec as P

TOP = 2
PAIR = 2
VMEM_LIMIT = 44 * 1024 * 1024
EXTRA_ROWS = 16
ROUTE_ROWS = 10
HIGH = lax.Precision.HIGHEST
F32 = jnp.float32
BF16 = jnp.bfloat16


def params():
    return pltpu.CompilerParams(vmem_limit_bytes=VMEM_LIMIT)


def cost(microseconds):
    return pl.CostEstimate(flops=0, bytes_accessed=int(microseconds * 3.69e6), transcendentals=0)


def after(array, *earlier):
    return lax.optimization_barrier((array,) + earlier)[0]


def swap_columns(array, distance):
    count = lax.axis_size("seq")
    return lax.ppermute(array, "seq", [(i, i ^ (PAIR * distance)) for i in range(count)])


def swap_cores(array):
    count = lax.axis_size("seq")
    return lax.ppermute(array, "seq", [(i, i ^ 1) for i in range(count)])


def swap_layers(array, distance):
    count = lax.axis_size("mp")
    return lax.ppermute(array, "mp", [(i, i ^ distance) for i in range(count)])


def local_kernel(column_ref, q_ref, k_ref, v_ref, decay_ref, residual_ref, local_ref, weighted_ref, *message_refs):
    span = q_ref.shape[0]
    heads = decay_ref.shape[0]
    size = q_ref.shape[1] // heads
    row = lax.broadcasted_iota(jnp.int32, (span, span), 0)
    col = lax.broadcasted_iota(jnp.int32, (span, span), 1)
    causal = row >= col
    decay = decay_ref[...]
    along = jnp.dot(decay, (row <= col).astype(F32), precision=HIGH, preferred_element_type=F32)
    down = lax.dot_general(
        causal.astype(F32), decay, (((1,), (1,)), ((), ())), precision=HIGH, preferred_element_type=F32
    )
    extra = lax.broadcasted_iota(jnp.int32, (EXTRA_ROWS, size), 0)
    for h in range(heads):
        cols = slice(h * size, (h + 1) * size)
        q, k, v = q_ref[:, cols], k_ref[:, cols], v_ref[:, cols]
        here = down[:, h : h + 1]
        spread = here - along[h : h + 1, :]
        weight = jnp.where(causal, jnp.exp(jnp.where(causal, spread, 0.0)), 0.0)
        raw = lax.dot_general(q, k, (((1,), (1,)), ((), ())), preferred_element_type=F32)
        local_ref[:, cols] = jnp.dot((raw * weight).astype(BF16), v, preferred_element_type=F32)
        total = along[h : h + 1, span - 1 : span]
        scaled = (jnp.exp(total - here) * k.astype(F32)).astype(BF16)
        state = lax.dot_general(scaled, v, (((0,), (0,)), ((), ())), preferred_element_type=F32).astype(BF16)
        first = total.astype(BF16).astype(F32)
        second = (total - first).astype(BF16).astype(F32)
        third = total - first - second
        pieces = jnp.where(extra == 0, first, jnp.where(extra == 1, second, jnp.where(extra == 2, third, 0.0)))
        at = h * (size + EXTRA_ROWS)
        for message in message_refs:
            message[at : at + size, :] = state
            message[at + size : at + size + EXTRA_ROWS, :] = pieces.astype(BF16)
        weighted_ref[:, cols] = (jnp.exp(here) * q.astype(F32)).astype(BF16)
    tok = residual_ref.shape[0]
    first = heads * (size + EXTRA_ROWS)
    for d, message in enumerate(message_refs):
        parts = (message.shape[0] - first) // tok
        for b in range(parts):
            at = pl.multiple_of((column_ref[d] * parts + b) * size, size)
            message[first + b * tok : first + (b + 1) * tok, :] = residual_ref[:, pl.ds(at, size)]


def prefix_kernel(count, heads, layers, *refs):
    row_ref, between_ref, earlier_ref, local_ref, weighted_ref, route_ref = refs[:6]
    message_refs = refs[6 : 6 + count]
    out_ref, totals, held = refs[6 + count :]
    span = local_ref.shape[0]
    size = local_ref.shape[1] // heads
    tall = size + EXTRA_ROWS
    for p in range(count):
        for h in range(heads):
            extra = message_refs[p][h * tall + size : (h + 1) * tall, :].astype(F32)
            totals[p : p + 1, h * size : (h + 1) * size] = jnp.sum(extra, axis=0, keepdims=True)
    gap = jnp.dot(between_ref[...], totals[...], precision=HIGH, preferred_element_type=F32)
    totals[...] = jnp.exp(gap) * earlier_ref[...]
    for h in range(heads):
        cols = slice(h * size, (h + 1) * size)
        prefix = jnp.zeros((size, size), F32)
        for p in range(count):
            prefix += totals[p : p + 1, cols] * message_refs[p][h * tall : h * tall + size, :].astype(F32)
        mixed = local_ref[:, cols] + jnp.dot(
            weighted_ref[:, cols], prefix.astype(BF16), preferred_element_type=F32
        )
        mean = jnp.mean(mixed * mixed, axis=-1, keepdims=True)
        held[:, cols] = (mixed * lax.rsqrt(mean + 1e-06)).astype(BF16)
    rows = span // layers
    for r in range(layers):
        start = pl.multiple_of(row_ref[r] * rows, rows)
        out_ref[r * rows : (r + 1) * rows, :] = held[pl.ds(start, rows), :]
    out_ref[span:, :] = jnp.zeros((EXTRA_ROWS, heads * size), BF16)
    out_ref[span:, :span] = route_ref[...]


def map_kernel(count, columns, capacity, tok, column_ref, *refs):
    row_refs, (pack_ref, high_ref, low_ref) = refs[:count], refs[count:]
    slots, span = high_ref.shape[0] // columns, high_ref.shape[1]
    row = lax.broadcasted_iota(jnp.int32, (slots, span), 0)
    lane = lax.broadcasted_iota(jnp.int32, (1, span), 1)
    base = (lane // tok) * capacity
    for p in range(count):
        route = row_refs[p][span : span + EXTRA_ROWS, :span].astype(F32)
        for d in range(columns):
            expert = column_ref[d]
            hit, gain = None, None
            for k in range(TOP):
                named = route[k : k + 1].astype(jnp.int32) == expert
                rank = route[TOP + k : TOP + k + 1].astype(jnp.int32)
                at = 2 * TOP + 3 * k
                value = route[at : at + 1] + route[at + 1 : at + 2] + route[at + 2 : at + 3]
                here = jnp.where(named, base + rank, -1) == row
                weight = jnp.where(here, value, 0.0)
                hit = here if hit is None else hit | here
                gain = weight if gain is None else gain + weight
            pack_ref[p, d * slots : (d + 1) * slots, :] = jnp.where(hit, 1.0, 0.0).astype(BF16)
            if p == 0:
                high = gain.astype(BF16)
                high_ref[d * slots : (d + 1) * slots, :] = high
                low_ref[d * slots : (d + 1) * slots, :] = (gain - high.astype(F32)).astype(BF16)


def project_kernel(count, layers, tok, core_ref, *refs):
    row_refs, message_refs = refs[:count], refs[count : 2 * count]
    weight_ref, keep_ref, send_ref = refs[2 * count :]
    span = layers * tok
    rows = jnp.concatenate([ref[:span] for ref in row_refs], axis=0)
    part = jnp.dot(rows, weight_ref[...], preferred_element_type=F32).astype(BF16)
    lanes = message_refs[0].shape[1]
    pieces = weight_ref.shape[1] // lanes
    for r in range(layers):
        for p in range(count):
            to = (r % (layers // 2)) * count * tok + p * tok
            here = part[p * span + r * tok : p * span + (r + 1) * tok]
            if r >= layers // 2:
                send_ref[to : to + tok, :] = here
            elif r > 0:
                keep_ref[to : to + tok, :] = here.astype(F32)
            else:
                for b in range(pieces):
                    own = message_refs[p][b * tok : (b + 1) * tok, :].astype(F32)
                    cols = slice(b * lanes, (b + 1) * lanes)
                    keep_ref[to : to + tok, cols] = here[:, cols].astype(F32) + own


def pack_kernel(count, layers, place_ref, map_ref, near_ref, far_ref, *out_refs):
    slots = out_refs[0].shape[0] // count
    tok = near_ref.shape[0] // (layers // 2) // count
    for p in range(count):
        pieces = [
            ref[r * count * tok + p * tok : r * count * tok + (p + 1) * tok, :]
            for ref in (near_ref, far_ref)
            for r in range(layers // 2)
        ]
        tokens = jnp.concatenate(pieces, axis=0)
        packed = jnp.dot(map_ref[p], tokens, preferred_element_type=F32).astype(BF16)
        start = pl.multiple_of(place_ref[p] * slots, slots)
        for d in range(len(out_refs)):
            out_refs[d][pl.ds(start, slots), :] = packed[d * slots : (d + 1) * slots]


def expert_kernel(pieces, blocks, first, last, features, place_ref, *refs):
    x_refs = refs[:pieces]
    gate_refs, up_refs = refs[pieces : pieces + blocks], refs[pieces + blocks : pieces + 2 * blocks]
    rest = refs[pieces + 2 * blocks :]
    if not first:
        sum_in, square_in = rest[:2]
        rest = rest[2:]
    if last:
        out_ref, sum_ref, square_ref = rest
    else:
        sum_ref, square_ref = rest
    size = gate_refs[0].shape[0]
    even = size // 128 * 128
    lanes = square_ref.shape[1]
    step = pl.program_id(0)

    for s in range(pieces // blocks):

        @pl.when(step == s)
        def _(s=s):
            x = jnp.concatenate([ref[...] for ref in x_refs[s * blocks : (s + 1) * blocks]], axis=1)
            gate = jnp.concatenate([ref[...] for ref in gate_refs], axis=1)
            up = jnp.concatenate([ref[...] for ref in up_refs], axis=1)
            both = jnp.concatenate([gate[:even], up[:even], gate[even:], up[even:]], axis=0)
            sums = lax.dot_general(x, both, (((1,), (1,)), ((), ())), preferred_element_type=F32)
            wide = x.astype(F32)
            squares = wide[:, :lanes] * wide[:, :lanes]
            for i in range(1, x.shape[1] // lanes):
                part = wide[:, i * lanes : (i + 1) * lanes]
                squares += part * part
            if s > 0:
                sum_ref[...] += sums
                square_ref[...] += squares
            else:
                sum_ref[...] = sums if first else sum_in[...] + sums
                square_ref[...] = squares if first else square_in[...] + squares

    if last:

        @pl.when(step == pl.num_programs(0) - 1)
        def _():
            slots = out_ref.shape[0] // pieces

            def activate(gate, up, scale):
                gate = gate * scale
                return (gate / (1.0 + jnp.exp(-gate)) * (up * scale)).astype(BF16)

            for p in range(pieces):
                rows = pl.ds(pl.multiple_of(place_ref[p] * slots, slots), slots)
                to = slice(p * slots, (p + 1) * slots)
                mean = jnp.sum(square_ref[rows, :], axis=1, keepdims=True) / features
                scale = lax.rsqrt(mean + 1e-06)
                out_ref[to, :even] = activate(sum_ref[rows, :even], sum_ref[rows, even : 2 * even], scale)
                if even < size:
                    tail = sum_ref[rows, 2 * even :]
                    out_ref[to, even:] = activate(tail[:, : size - even], tail[:, size - even :], scale)


def down_kernel(hidden_ref, weight_ref, own_ref, *other_refs):
    half = own_ref.shape[0]
    out = jnp.dot(hidden_ref[...], weight_ref[...], preferred_element_type=F32).astype(BF16)
    own_ref[...] = out[:half]
    rows = half // len(other_refs)
    for d, ref in enumerate(other_refs):
        ref[...] = out[half + d * rows : half + (d + 1) * rows]


def combine_kernel(count, high_ref, low_ref, *refs):
    x_refs = refs[:count]
    keep_ref, send_ref = refs[count:]
    half = keep_ref.shape[0]
    x = jnp.concatenate([ref[...] for ref in x_refs], axis=0)
    out = lax.dot_general(high_ref[...], x, (((0,), (0,)), ((), ())), preferred_element_type=F32)
    out += lax.dot_general(low_ref[...], x, (((0,), (0,)), ((), ())), preferred_element_type=F32)
    keep_ref[...] = out[:half]
    send_ref[...] = out[half:].astype(BF16)


def whole_block(array):
    return pl.BlockSpec(array.shape, lambda *_: (0,) * array.ndim)


def tiled(
    queries, keys, values, log_decay, residual, out_weight, gate_weight, up_weight, down_weight, expert_ids,
    route_weights, chunks, returns,
):
    seq_count, layers = lax.axis_size("seq"), lax.axis_size("mp")
    me, layer = lax.axis_index("seq"), lax.axis_index("mp")
    columns = seq_count // PAIR
    column = me // PAIR
    span, heads = queries.shape[0], log_decay.shape[0]
    size = queries.shape[1] // heads
    features = residual.shape[1]
    hidden_size = gate_weight.shape[2]
    tok = residual.shape[0]
    half = span // 2
    block = out_weight.shape[1]
    width = block // chunks
    capacity = max(2, tok * TOP * 3 // (2 * columns))
    slots = layers * capacity
    distances = [1 << i for i in range((layers - 1).bit_length())]
    order = [0]
    for d in reversed(distances):
        order = order + [b ^ d for b in order]

    away = [PAIR * (p % columns) + p // columns for p in range(seq_count)]
    blocks_at = jnp.stack([me ^ a for a in away]).astype(jnp.int32)
    rows_at = jnp.stack([layer ^ r for r in order]).astype(jnp.int32)
    columns_at = jnp.stack([column ^ d for d in range(columns)]).astype(jnp.int32)

    def across(array):
        return [array] + [swap_columns(array, d) for d in range(1, columns)]

    def both_cores(arrays):
        arrays = list(arrays)
        return arrays + [swap_cores(a) for a in arrays]

    smem = pl.BlockSpec(memory_space=pltpu.SMEM)
    vmem = pl.BlockSpec(memory_space=pltpu.VMEM)
    residual_at = heads * (size + EXTRA_ROWS)
    message = (residual_at + PAIR * block // size * tok, size)
    local_part, weighted_queries, *messages = pl.pallas_call(
        local_kernel,
        out_shape=(
            jax.ShapeDtypeStruct((span, heads * size), F32),
            jax.ShapeDtypeStruct((span, heads * size), BF16),
        )
        + (jax.ShapeDtypeStruct(message, BF16),) * columns,
        grid=(1,),
        in_specs=[smem] + [whole_block(a) for a in (queries, keys, values, log_decay, residual)],
        out_specs=(pl.BlockSpec((span, heads * size), lambda n: (0, 0)),) * 2
        + (pl.BlockSpec(message, lambda n: (0, 0)),) * columns,
        compiler_params=params(),
        cost_estimate=cost(1.5),
        name="local_attention",
    )(columns_at, queries, keys, values, log_decay, residual)
    messages = [messages[0]] + [swap_columns(messages[d], d) for d in range(1, columns)]

    flat = after(expert_ids, local_part).reshape(-1)
    count = flat.shape[0]
    before = jnp.arange(count)[:, None] > jnp.arange(count)[None, :]
    rank = jnp.sum((before & (flat[:, None] == flat[None, :])).astype(jnp.int32), axis=1).reshape(tok, TOP)
    first = lax.reduce_precision(route_weights, 8, 7)
    second = lax.reduce_precision(route_weights - first, 8, 7)
    third = route_weights - first - second
    parts = jnp.stack([first, second, third], axis=2).reshape(tok, 3 * TOP)
    route = jnp.concatenate([expert_ids.astype(F32), rank.astype(F32), parts], axis=1).T.astype(BF16)
    route = jnp.pad(route, ((0, EXTRA_ROWS - ROUTE_ROWS), (0, 0)))
    for d in reversed(distances):
        route = jnp.concatenate([route, swap_layers(route, d)], axis=1)

    messages = both_cores([after(a, route) for a in messages])
    between = ((blocks_at[:, None] < blocks_at[None, :]) & (blocks_at[None, :] < me)).astype(F32)
    earlier = jnp.broadcast_to((blocks_at < me).astype(F32)[:, None], (seq_count, heads * size))
    normed = pl.pallas_call(
        functools.partial(prefix_kernel, seq_count, heads, layers),
        out_shape=jax.ShapeDtypeStruct((span + EXTRA_ROWS, heads * size), BF16),
        in_specs=[smem] + [vmem] * (5 + seq_count),
        out_specs=vmem,
        scratch_shapes=[pltpu.VMEM((seq_count, heads * size), F32), pltpu.VMEM((span, heads * size), BF16)],
        compiler_params=params(),
        cost_estimate=cost(1.2),
        name="prefix_attention",
    )(rows_at, between, earlier, local_part, weighted_queries, route, *messages)
    normed = both_cores(across(normed))

    core = me % PAIR
    core_at = (residual_at + core * (block // size * tok)).reshape(1).astype(jnp.int32)

    def slot_maps(*earlier):
        return pl.pallas_call(
            functools.partial(map_kernel, seq_count, columns, capacity, tok),
            out_shape=(
                jax.ShapeDtypeStruct((seq_count, columns * slots, span), BF16),
                jax.ShapeDtypeStruct((columns * slots, span), BF16),
                jax.ShapeDtypeStruct((columns * slots, span), BF16),
            ),
            in_specs=[smem] + [vmem] * seq_count,
            out_specs=(vmem,) * 3,
            compiler_params=params(),
            cost_estimate=cost(1.3),
            name="slot_maps",
        )(columns_at, after(normed[0], *earlier), *normed[1:])

    rows = seq_count * slots
    summed_rows = seq_count * half
    gate_view, up_view = gate_weight[0].T, up_weight[0].T

    own_rows = width // size * tok

    def project(i, *earlier):
        keep, send = pl.pallas_call(
            functools.partial(project_kernel, seq_count, layers, tok),
            out_shape=(
                jax.ShapeDtypeStruct((summed_rows, width), F32),
                jax.ShapeDtypeStruct((summed_rows, width), BF16),
            ),
            grid_spec=pltpu.PrefetchScalarGridSpec(
                num_scalar_prefetch=1,
                grid=(1,),
                in_specs=[whole_block(a) for a in normed]
                + [pl.BlockSpec((own_rows, size), lambda n, at: (at[0] // own_rows + i, 0))] * seq_count
                + [pl.BlockSpec((heads * size, width), lambda n, at: (0, i))],
                out_specs=(pl.BlockSpec((summed_rows, width), lambda n, at: (0, 0)),) * 2,
            ),
            compiler_params=params(),
            cost_estimate=cost(1),
            name="project",
        )(core_at, after(normed[0], *earlier), *normed[1:], *messages, out_weight)
        return keep, swap_layers(send, distances[0])

    def sum_layers(keep, arrived):
        part = (keep + arrived.astype(F32)).astype(BF16)
        return part, swap_layers(part, distances[-1])

    def add_layers(part, other):
        middle = other.shape[0] // 2
        other = jnp.concatenate([other[middle:], other[:middle]], axis=0)
        token = (part.astype(F32) + other.astype(F32)).astype(BF16)
        return token, swap_layers(token, distances[0])

    def dispatch(token, far):
        packed = pl.pallas_call(
            functools.partial(pack_kernel, seq_count, layers),
            out_shape=(jax.ShapeDtypeStruct((rows, width), BF16),) * columns,
            in_specs=[smem] + [vmem] * 3,
            out_specs=(vmem,) * columns,
            compiler_params=params(),
            cost_estimate=cost(1),
            name="pack",
        )(blocks_at, pack_map, token, far)
        return [packed[0]] + [swap_columns(packed[d], d) for d in range(1, columns)]

    blocks = columns
    sum_shapes = ((rows, 2 * hidden_size), (rows, 128))

    def gate_up(i, arrived, held):
        first, last = i == 0, i == chunks - 1

        def weight_block(b):
            return pl.BlockSpec((hidden_size, width), lambda s, at: (0, at[s * blocks + b] * chunks + i))

        def constant(shape):
            return pl.BlockSpec(shape, lambda s, at: (0, 0))

        return pl.pallas_call(
            functools.partial(expert_kernel, seq_count, blocks, first, last, features),
            grid_spec=pltpu.PrefetchScalarGridSpec(
                num_scalar_prefetch=1,
                grid=(seq_count // blocks,),
                in_specs=[constant((rows, width))] * seq_count
                + [weight_block(b) for b in range(blocks)] * 2
                + [constant(a.shape) for a in held],
                out_specs=constant((rows, hidden_size)) if last else tuple(constant(s) for s in sum_shapes),
                scratch_shapes=[pltpu.VMEM(s, F32) for s in sum_shapes] if last else [],
            ),
            out_shape=jax.ShapeDtypeStruct((rows, hidden_size), BF16)
            if last
            else tuple(jax.ShapeDtypeStruct(s, F32) for s in sum_shapes),
            compiler_params=params(),
            cost_estimate=cost(24 / chunks),
            name="gate_up",
        )(blocks_at, *arrived, *[gate_view] * blocks, *[up_view] * blocks, *held)

    projected, sent, tokens, arrived, sums = [None] * chunks, [None] * chunks, [None] * chunks, [None] * chunks, []
    projected[0] = project(0)
    sent[0] = sum_layers(*projected[0])
    pack_map, mix_high, mix_low = slot_maps(sent[0][0])
    for i in range(chunks):
        if i + 1 < chunks:
            projected[i + 1] = project(i + 1, sent[i][0])
        if i == chunks - 1:
            both = both_cores(after(a, sent[i][0]) for a in arrived[0])
            sums = gate_up(0, both, sums)
            sent[i] = (after(sent[i][0], *sums), sent[i][1])
        tokens[i] = add_layers(*sent[i])
        if i + 1 < chunks:
            sent[i + 1] = sum_layers(*projected[i + 1])
        arrived[i] = dispatch(*tokens[i])
    middle = summed_rows // 2
    own = jnp.concatenate([token[:middle] for token, _ in tokens], axis=1)
    other = swap_cores(own[middle // 2 :])
    own = own[: middle // 2]
    joined = jnp.where(core == 0, jnp.concatenate([own, other], axis=1), jnp.concatenate([other, own], axis=1))
    joined = [joined[d * tok : (d + 1) * tok] for d in range(columns)]
    for i in range(1, chunks):
        both = both_cores([after(a, *sums) for a in arrived[i]])
        if i == chunks - 1:
            joined = [after(a, *arrived[i]) for a in joined]
            both[0] = after(both[0], *joined)
            joined = [joined[0]] + [swap_columns(joined[d], d) for d in range(1, columns)]
        sums = gate_up(i, both, sums)
    expert_hidden = after(sums, *joined)
    tile = 1024

    def down(piece, *earlier):
        offset, out_width = piece
        own, *other = pl.pallas_call(
            down_kernel,
            grid=(out_width // tile,),
            out_shape=(jax.ShapeDtypeStruct((rows // 2, out_width), BF16),)
            + (jax.ShapeDtypeStruct((slots, out_width), BF16),) * columns,
            in_specs=[
                whole_block(expert_hidden),
                pl.BlockSpec((hidden_size, tile), lambda n: (0, offset // tile + n)),
            ],
            out_specs=(pl.BlockSpec((rows // 2, tile), lambda n: (0, n)),)
            + (pl.BlockSpec((slots, tile), lambda n: (0, n)),) * columns,
            compiler_params=params(),
            cost_estimate=cost(16 * out_width / features),
            name="down",
        )(after(expert_hidden, *earlier), down_weight[0])
        return own, [swap_cores(a) for a in other]

    def summed(own, other, *earlier):
        own = after(own, *earlier)
        return [
            (own[d * slots : (d + 1) * slots].astype(F32) + other[d].astype(F32)).astype(BF16)
            for d in range(columns)
        ]

    def combine(piece, back):
        out_width = piece[1]
        keep, send = pl.pallas_call(
            functools.partial(combine_kernel, columns),
            grid=(out_width // tile,),
            out_shape=(
                jax.ShapeDtypeStruct((half, out_width), F32),
                jax.ShapeDtypeStruct((half, out_width), BF16),
            ),
            in_specs=[whole_block(mix_high), whole_block(mix_low)]
            + [pl.BlockSpec((slots, tile), lambda n: (0, n))] * columns,
            out_specs=(pl.BlockSpec((half, tile), lambda n: (0, n)),) * 2,
            compiler_params=params(),
            cost_estimate=cost(1),
            name="combine",
        )(mix_high, mix_low, *back)
        return keep, swap_layers(send, distances[0])

    def layer_sum(keep, arrived):
        part = keep + arrived.astype(F32)
        kept = part.shape[0] // 2
        return part[:kept], swap_layers(part[kept:].astype(BF16), distances[-1])

    def finish(piece, part, arrived):
        mine = own_hidden[:, piece[0] : piece[0] + piece[1]].astype(F32)
        return (mine + (part + arrived.astype(F32))).astype(BF16)

    sent, mixed, last = [], [], []
    ahead = down(returns[0])
    for i, piece in enumerate(returns):
        sums = summed(*ahead, *(sent[i - 1] if i else []))
        sent.append([sums[0]] + [swap_columns(sums[d], d) for d in range(1, columns)])
        if i + 1 < len(returns):
            ahead = down(returns[i + 1], *sums)
        if i:
            gate = ahead[1] if i + 1 < len(returns) else sums
            mixed.append(combine(returns[i - 1], [after(a, *gate) for a in sent[i - 1]]))
    earlier = []
    for i in range(len(returns) - 1):
        last.append(layer_sum(mixed[i][0], after(mixed[i][1], *earlier)))
        earlier = [last[i][1]] if i + 2 < len(returns) else [last[i][0]]
    mixed.append(combine(returns[-1], [after(a, *earlier) for a in sent[-1]]))
    last.append(layer_sum(*mixed[-1]))

    joined = jnp.concatenate(joined, axis=0)
    own_hidden = jnp.concatenate(
        [lax.dynamic_slice_in_dim(joined, columns_at[d] * tok, tok, 0) for d in range(columns)], axis=1
    )
    outputs = [finish(piece, *last[i]) for i, piece in enumerate(returns)]
    return jnp.concatenate(outputs, axis=1)


def general(
    queries,
    keys,
    values,
    log_decay,
    residual,
    out_weight,
    gate_weight,
    up_weight,
    down_weight,
    expert_ids,
    route_weights,
):
    seq_count = lax.axis_size("seq")
    span_len = queries.shape[0]
    head_count = log_decay.shape[0]
    head_size = queries.shape[1] // head_count
    query_heads = queries.reshape(span_len, head_count, head_size)
    key_heads = keys.reshape(span_len, head_count, head_size)
    value_heads = values.reshape(span_len, head_count, head_size)
    cumulative = jnp.cumsum(log_decay, axis=1)
    positions = jnp.arange(span_len)
    causal = (positions[:, None] >= positions[None, :])[None]
    spread_log = cumulative[:, :, None] - cumulative[:, None, :]
    weight = jnp.where(causal, jnp.exp(jnp.where(causal, spread_log, 0.0)), 0.0)
    raw_scores = jnp.einsum(
        "thd,shd->hts", query_heads, key_heads, preferred_element_type=jnp.float32
    )
    local_scores = (raw_scores * weight).astype(jnp.bfloat16)
    local_part = jnp.einsum(
        "hts,shd->thd", local_scores, value_heads, preferred_element_type=jnp.float32
    )
    span_total = cumulative[:, -1]
    key_scale = jnp.exp(span_total[:, None] - cumulative)
    weighted_keys = (key_scale.T[:, :, None] * key_heads.astype(jnp.float32)).astype(jnp.bfloat16)
    span_state = jnp.einsum(
        "thd,the->hde", weighted_keys, value_heads, preferred_element_type=jnp.float32
    ).astype(jnp.bfloat16)
    decays = lax.all_gather(span_total[None, :], "seq", axis=0, tiled=True)
    running = jnp.cumsum(decays, axis=0)
    my_index = lax.axis_index("seq")
    before = lax.dynamic_index_in_dim(running, jnp.maximum(my_index - 1, 0), 0, keepdims=False)
    shard_piece = lax.all_gather(span_state[None], "seq", axis=0, tiled=True)
    row_count = shard_piece.shape[0]
    source = jnp.arange(row_count)
    earlier_mask = (source < my_index)[:, None]
    factor = jnp.where(
        earlier_mask, jnp.exp(jnp.where(earlier_mask, before[None, :] - running, 0.0)), 0.0
    )
    prefix = jnp.einsum(
        "nh,nhde->hde", factor, shard_piece.astype(jnp.float32), precision=lax.Precision.HIGHEST
    )
    prefix_low = prefix.astype(jnp.bfloat16)
    weighted_queries = (jnp.exp(cumulative).T[:, :, None] * query_heads.astype(jnp.float32)).astype(
        jnp.bfloat16
    )
    carried_part = jnp.einsum(
        "thd,hde->the", weighted_queries, prefix_low, preferred_element_type=jnp.float32
    )
    mixed_heads = local_part + carried_part
    normed = (
        mixed_heads * lax.rsqrt(jnp.mean(mixed_heads * mixed_heads, axis=-1, keepdims=True) + 1e-06)
    ).astype(jnp.bfloat16)
    normed = normed.reshape(span_len, head_count * head_size)
    partial_out = jnp.dot(
        normed,
        lax.all_gather(out_weight, "seq", axis=1, tiled=True),
        preferred_element_type=jnp.float32,
    )
    attn_out = lax.psum_scatter(
        partial_out.astype(jnp.bfloat16), "mp", scatter_dimension=0, tiled=True
    ).astype(jnp.float32)
    hidden_state = (residual.astype(jnp.float32) + attn_out).astype(jnp.bfloat16)
    hidden_wide = hidden_state.astype(jnp.float32)
    moe_input = (
        hidden_wide * lax.rsqrt(jnp.mean(hidden_wide * hidden_wide, axis=-1, keepdims=True) + 1e-06)
    ).astype(jnp.bfloat16)
    model_width = residual.shape[1]
    experts = seq_count // PAIR
    tok_rows = residual.shape[0]
    capacity = max(2, tok_rows * TOP * 3 // (2 * experts))
    assign_count = tok_rows * TOP
    flat_ids = expert_ids.reshape(-1)
    expert_hot = (flat_ids[:, None] == jnp.arange(experts)[None, :]).astype(jnp.int32)
    slot_rank = jnp.sum((jnp.cumsum(expert_hot, axis=0) - expert_hot) * expert_hot, axis=1)
    target = flat_ids * capacity + slot_rank
    slot_hot = (target[:, None] == jnp.arange(experts * capacity)[None, :]).astype(jnp.float32)
    owner_hot = (
        (jnp.arange(assign_count) // TOP)[:, None] == jnp.arange(tok_rows)[None, :]
    ).astype(jnp.float32)
    dispatch_map = jnp.einsum("as,at->st", slot_hot, owner_hot).astype(jnp.bfloat16)
    packed = jnp.dot(dispatch_map, moe_input, preferred_element_type=jnp.float32).astype(
        jnp.bfloat16
    )
    outgoing = jnp.broadcast_to(
        packed.reshape(experts, 1, capacity, model_width), (experts, PAIR, capacity, model_width)
    )
    outgoing = outgoing.reshape(seq_count, capacity, model_width)
    incoming = lax.all_to_all(outgoing, "seq", split_axis=0, concat_axis=0, tiled=True)
    expert_rows = incoming.reshape(seq_count * capacity, model_width)
    gate_matrix = gate_weight[0]
    up_matrix = up_weight[0]
    down_matrix = down_weight[0]
    shard_piece = lax.all_gather(expert_rows, "mp", axis=0, tiled=True)
    gate_value = jnp.dot(shard_piece, gate_matrix, preferred_element_type=jnp.float32)
    lifted = jnp.dot(shard_piece, up_matrix, preferred_element_type=jnp.float32)
    hidden_rows = (jax.nn.silu(gate_value) * lifted).astype(jnp.bfloat16)
    half_out = lax.psum_scatter(
        jnp.dot(hidden_rows, down_matrix, preferred_element_type=jnp.float32).astype(jnp.bfloat16),
        "mp",
        scatter_dimension=0,
        tiled=True,
    )
    returned = lax.all_to_all(
        half_out.reshape(seq_count, capacity, model_width),
        "seq",
        split_axis=0,
        concat_axis=0,
        tiled=True,
    )
    expert_out = jnp.sum(
        returned.reshape(experts, PAIR, capacity, model_width).astype(jnp.float32), axis=1
    )
    expert_out = expert_out.reshape(experts * capacity, model_width)
    weighted = route_weights.reshape(-1)[:, None] * slot_hot
    combine_map = jnp.einsum("at,as->ts", owner_hot, weighted, precision=lax.Precision.HIGHEST)
    expert_mix = jnp.dot(combine_map, expert_out, precision=lax.Precision.HIGHEST)
    return (hidden_wide + expert_mix).astype(jnp.bfloat16)


def cuts(tile, parts):
    return [(sum(parts[:i]) * tile, part * tile) for i, part in enumerate(parts)]


def fits(mesh, tok, features, block, chunks, heads):
    layers, seq_count = mesh.shape["mp"], mesh.shape["seq"]
    powers = seq_count & (seq_count - 1) == 0 and seq_count > PAIR
    if block % (128 * chunks) or heads * (128 + EXTRA_ROWS) % (block // (128 * chunks) * tok):
        return False
    return powers and layers == 4 and tok % 16 == 0 and features % (512 * 12) == 0


def solution(mesh):
    placed = (
        P("seq", "mp"),
        P("seq", "mp"),
        P("seq", "mp"),
        P("mp", "seq"),
        P(("seq", "mp"), None),
        P("mp", "seq"),
        P("seq", None, "mp"),
        P("seq", None, "mp"),
        P("seq", "mp", None),
        P(("seq", "mp"), None),
        P(("seq", "mp"), None),
    )
    chunks = 3

    def per_device(*args):
        residual, out_weight = args[4], args[5]
        features, block = residual.shape[1], out_weight.shape[1]
        if fits(mesh, residual.shape[0], features, block, chunks, args[3].shape[0]):
            return tiled(*args, chunks=chunks, returns=cuts(features // 12, [2, 4, 4, 2]))
        return general(*args)

    return jax.shard_map(
        per_device, mesh=mesh, in_specs=placed, out_specs=P(("seq", "mp"), None), check_vma=False
    )
```
